512 devices in a mesh: section: 8 (over x, core), dp: 64 (over z, y).
Axes of the slice: x: 4, y: 4, z: 16, core: 2. Of those that a mesh axis runs over, the one named last changes fastest.
Arguments:
- teacher_hidden: bfloat16 [256, 8192], P('dp'), may hold values from -12 to 12
- student_hidden: bfloat16 [256, 3584], P('dp'), may hold values from -12 to 12
- teacher_gain: bfloat16 [8192], replicated, may hold values from 0.5 to 1.5
- student_gain: bfloat16 [3584], replicated, may hold values from 0.5 to 1.5
- teacher_head: bfloat16 [81920, 8192], P(('section', 'dp')), may hold values from -64 to 64
- student_head: bfloat16 [81920, 3584], P(('section', 'dp')), may hold values from -64 to 64
- labels: int32 [256], replicated, may hold values from 0 to 81919
- cotangent: float32 [256], replicated, may hold values from 2 to 20
Outputs:
- loss: float32 [], replicated
- student_grad: float32 [256, 3584], P('dp')
- gain_grad: float32 [3584], replicated
- head_grad: bfloat16 [81920, 3584], P(('section', 'dp'))
The draws below stay inside these ranges and needn't reach their ends.
All inputs are finite; a program needn't handle non-finite values.
Results may differ from the reference program's by a relative error of at most 0.0079.
Values may be sent and summed in bfloat16 or wider, within the bound.
No kernel may reach another device: no remote copies, remote signals or barrier semaphores. Data moves between devices by JAX's collectives and lax.ppermute only.
A program may use at most 64 MiB of HBM per device.

```python
import math
import jax
import jax.numpy as jnp
from jax import lax

DT = 8192
DS = 3584
TOKENS = 256
VOCAB = 81920


def unit_column(head_key, index, width):
    return jnp.clip(jax.random.normal(jax.random.fold_in(head_key, index), (width,), jnp.float32), -5.0, 5.0)


def chosen_rows(pick_key):
    return jax.random.randint(pick_key, (8, 2), 0, VOCAB)


def head_block(head_key, width, pick_key):
    rows = jax.vmap(lambda index: unit_column(head_key, index, width))(jnp.arange(VOCAB))
    boost = max(1.0, 90.0 / float(width) ** 0.5)
    picks = chosen_rows(pick_key).reshape(-1)
    marked = jnp.any(jnp.arange(VOCAB)[:, None] == picks[None, :], axis=1)
    factor = jnp.where(marked, boost, 1.0).astype(jnp.float32)[:, None]
    return rows * factor * (4.0 / jnp.sqrt(jnp.float32(width)))


def aligned_hidden(noise_key, width, head_key, pick_key):
    base = jnp.clip(jax.random.normal(noise_key, (TOKENS, width), jnp.float32), -6.0, 6.0)
    picks = chosen_rows(pick_key)
    first = jax.vmap(lambda index: unit_column(head_key, index, width))(picks[:, 0])
    second = jax.vmap(lambda index: unit_column(head_key, index, width))(picks[:, 1])
    strength = jnp.array([1.0, 0.9, 0.8, 0.7, 1.0, 0.9, 0.8, 0.7], jnp.float32)[:, None]
    rows = strength * (first + 0.99 * second) / 1.41 + jnp.sqrt(1.0 - strength * strength) * base[-8:]
    base = base.at[-8:].set(rows)
    return jnp.clip(base, -12.0, 12.0)


def draw_teacher_head(key, part):
    return head_block(jax.random.fold_in(key, 101), DT, jax.random.fold_in(key, 303)).astype(jnp.bfloat16)


def draw_student_head(key, part):
    return head_block(jax.random.fold_in(key, 202), DS, jax.random.fold_in(key, 404)).astype(jnp.bfloat16)


def draw_teacher_hidden(key, part):
    return aligned_hidden(jax.random.fold_in(key, 11), DT, jax.random.fold_in(key, 101), jax.random.fold_in(key, 303)).astype(jnp.bfloat16)


def draw_student_hidden(key, part):
    return aligned_hidden(jax.random.fold_in(key, 12), DS, jax.random.fold_in(key, 202), jax.random.fold_in(key, 404)).astype(jnp.bfloat16)


def place_ends(drawn, key, low, top_value):
    index_at = [jax.random.randint(jax.random.fold_in(key, axis), (), 0, length) for axis, length in enumerate(drawn.shape)]
    longest = drawn.shape.index(max(drawn.shape))
    beside = index_at[:longest] + [(index_at[longest] + 1) % drawn.shape[longest]] + index_at[longest + 1:]
    return drawn.at[tuple(index_at)].set(low).at[tuple(beside)].set(top_value)


def setup_inputs(seed: int = 0) -> dict:
    key_of = jax.random.split(jax.random.key(seed), 9)
    return {
        "teacher_hidden": draw_teacher_hidden(jax.random.fold_in(key_of[8], 71), 0),
        "student_hidden": draw_student_hidden(jax.random.fold_in(key_of[8], 71), 0),
        "teacher_gain": jnp.clip(1.0 + 0.1 * jax.random.normal(key_of[2], (DT,), jnp.float32), 0.5, 1.5).astype(jnp.bfloat16),
        "student_gain": jnp.clip(1.0 + 0.1 * jax.random.normal(key_of[3], (DS,), jnp.float32), 0.5, 1.5).astype(jnp.bfloat16),
        "teacher_head": draw_teacher_head(jax.random.fold_in(key_of[8], 71), 0),
        "student_head": draw_student_head(jax.random.fold_in(key_of[8], 71), 0),
        "labels": place_ends(jax.random.randint(key_of[6], (TOKENS,), 0, VOCAB), jax.random.fold_in(key_of[6], 1), 0, VOCAB - 1).astype(jnp.int32),
        "cotangent": jnp.clip(jnp.exp(jax.random.uniform(key_of[7], (TOKENS,), jnp.float32, math.log(2.0), math.log(20.0))), 2.0, 20.0),
    }


eps = 1e-06
ce_weight = 0.5

def normalize(hidden, gain):
    values = hidden.astype(jnp.float32)
    inverse = lax.rsqrt(lax.optimization_barrier(jnp.mean(values * values, axis=-1, keepdims=True)) + eps)
    scaled = values * inverse
    return (scaled, inverse, (scaled * gain.astype(jnp.float32)).astype(jnp.bfloat16))

def reference(teacher_hidden, student_hidden, teacher_gain, student_gain, teacher_head, student_head, labels, cotangent):
    _, _, teacher_normed = normalize(teacher_hidden, teacher_gain)
    scaled, inverse, student_normed = normalize(student_hidden, student_gain)
    teacher_logits = lax.dot_general(teacher_normed, teacher_head, (((1,), (1,)), ((), ())), preferred_element_type=jnp.float32)
    student_logits = lax.dot_general(student_normed, student_head, (((1,), (1,)), ((), ())), preferred_element_type=jnp.float32)
    teacher_peak = lax.optimization_barrier(jnp.max(teacher_logits, axis=1, keepdims=True))
    student_peak = lax.optimization_barrier(jnp.max(student_logits, axis=1, keepdims=True))
    teacher_exp = jnp.exp(teacher_logits - teacher_peak)
    teacher_total = lax.optimization_barrier(jnp.sum(teacher_exp, axis=1, keepdims=True))
    cross = lax.optimization_barrier(jnp.sum(teacher_exp * (teacher_logits - student_logits), axis=1, keepdims=True))
    student_total = lax.optimization_barrier(jnp.sum(jnp.exp(student_logits - student_peak), axis=1, keepdims=True))
    columns = lax.broadcasted_iota(jnp.int32, student_logits.shape, 1)
    hits = columns == labels.astype(jnp.int32)[:, None]
    picked = lax.optimization_barrier(jnp.sum(jnp.where(hits, student_logits, 0.0), axis=1, keepdims=True))
    teacher_log = teacher_peak + jnp.log(teacher_total)
    student_log = student_peak + jnp.log(student_total)
    token_loss = cross / teacher_total - teacher_log + student_log + ce_weight * (student_log - picked)
    loss = jnp.mean(token_loss)
    student_prob = jnp.exp(student_logits - student_log)
    teacher_prob = jnp.exp(teacher_logits - teacher_log)
    onehot = jnp.where(hits, 1.0, 0.0).astype(jnp.float32)
    slope = (cotangent[:, None] * ((1.0 + ce_weight) * student_prob - teacher_prob - ce_weight * onehot)).astype(jnp.bfloat16)
    head_grad = lax.dot_general(slope, student_normed, (((0,), (0,)), ((), ())), preferred_element_type=jnp.float32).astype(jnp.bfloat16)
    normed_grad = jnp.dot(slope, student_head, preferred_element_type=jnp.float32)
    gain_grad = lax.optimization_barrier(jnp.sum(normed_grad * scaled, axis=0))
    weighted = normed_grad * student_gain.astype(jnp.float32)
    student_grad = inverse * (weighted - scaled * lax.optimization_barrier(jnp.mean(weighted * scaled, axis=1, keepdims=True)))
    return (loss, student_grad, gain_grad, head_grad)
```

```python
import jax
import jax.numpy as jnp
from jax import lax
from jax.sharding import Mesh
from jax.sharding import PartitionSpec as P

X, C, Z, Y = ("section_0", "section_1", "dp_0", "dp_1")
DP = (Z, Y)
SECTION_DP = (X, C, Z, Y)
PLANE = (X, Y)

eps = 1e-06
ce_weight = 0.5
f32 = jnp.float32
bf16 = jnp.bfloat16


def to_all(x, axes):
    length = lax.axis_size(axes)
    return lax.all_to_all(jnp.broadcast_to(x[None], (length, *x.shape)), axes, 0, 0, tiled=True)


def swapped(x):
    return lax.ppermute(x, C, [(0, 1), (1, 0)])


def normalize(hidden):
    values = hidden.astype(f32)
    inverse = lax.rsqrt(jnp.mean(values * values, axis=-1, keepdims=True) + eps)
    return (values * inverse, inverse)


def merged(logs):
    peak = jnp.max(logs, axis=0)
    return peak + jnp.log(jnp.sum(jnp.exp(logs - peak[None]), axis=0))


def high_low(x):
    high = x.astype(bf16)
    return (high, (x - high.astype(f32)).astype(bf16))


def dot(a, b, along_a, along_b):
    return lax.dot_general(a, b, (((along_a,), (along_b,)), ((), ())), preferred_element_type=f32)


def on_device(
    teacher_hidden,
    student_hidden,
    teacher_gain,
    student_gain,
    teacher_head,
    student_head,
    labels,
    cotangent,
):
    nx, nc, nz, ny = (lax.axis_size(a) for a in SECTION_DP)
    ix, ic, iz, iy = (lax.axis_index(a) for a in SECTION_DP)
    rows, dt = teacher_head.shape
    ds = student_head.shape[1]
    own = teacher_hidden.shape[0]
    half = own // nc
    qt, qs = (dt // nx, ds // nx)
    held = nz * half
    tokens = ny * held

    teacher_other, student_other = (swapped(teacher_head), swapped(student_head))

    t_scaled, _ = normalize(lax.dynamic_slice_in_dim(teacher_hidden, ic * half, half, 0))
    scaled, inverse = normalize(student_hidden)
    s_scaled = lax.dynamic_slice_in_dim(scaled, ic * half, half, 0)
    t_part = lax.dynamic_slice_in_dim(t_scaled, ix * qt, qt, 1)
    s_part = lax.dynamic_slice_in_dim(s_scaled, ix * qs, qs, 1)
    t_gain = lax.dynamic_slice_in_dim(teacher_gain, ix * qt, qt, 0).astype(f32)
    s_gain = lax.dynamic_slice_in_dim(student_gain, ix * qs, qs, 0).astype(f32)
    piece = jnp.concatenate(
        [(t_part * t_gain).astype(bf16), (s_part * s_gain).astype(bf16)], axis=1
    )
    line = to_all(piece, Z).reshape(held, qt + qs)
    plane = to_all(line, PLANE).reshape(nx, tokens, qt + qs)
    teacher_rows = jnp.concatenate([plane[k, :, :qt] for k in range(nx)], axis=1)
    student_rows = jnp.concatenate([plane[k, :, qt:] for k in range(nx)], axis=1)
    student_rows_other = swapped(student_rows)

    t_logits = jnp.concatenate(
        [dot(teacher_head, teacher_rows, 1, 1), dot(teacher_other, teacher_rows, 1, 1)], axis=0
    )
    s_logits = jnp.concatenate(
        [dot(student_head, student_rows, 1, 1), dot(student_other, student_rows, 1, 1)], axis=0
    )

    def local_log(logits):
        peak = jnp.max(logits, axis=0)
        return peak + jnp.log(jnp.sum(jnp.exp(logits - peak[None]), axis=0))

    logs = jnp.stack([local_log(t_logits), local_log(s_logits)])
    logs = merged(to_all(logs, PLANE))
    logs = merged(to_all(logs, Z))
    teacher_log, student_log = (logs[0], logs[1])

    def of_tokens(a):
        mine = lax.dynamic_index_in_dim(a.reshape(nz, ny, nc, half), ic, 2, keepdims=False)
        return mine.transpose(1, 0, 2).reshape(tokens)

    label, cot = (of_tokens(labels), of_tokens(cotangent))

    def start_of(core):
        return (((ix * nc + core) * nz + iz) * ny + iy) * rows

    first = lax.broadcasted_iota(jnp.int32, (rows, tokens), 0)
    entry = jnp.concatenate([first + start_of(ic), first + start_of(1 - ic)], axis=0)
    hits = entry == label[None, :]
    student_prob = jnp.exp(s_logits - student_log[None])
    teacher_prob = jnp.exp(t_logits - teacher_log[None])
    onehot = jnp.where(hits, 1.0, 0.0).astype(f32)
    slope = (
        cot[None] * ((1.0 + ce_weight) * student_prob - teacher_prob - ce_weight * onehot)
    ).astype(bf16)
    loss_part = jnp.sum(
        teacher_prob * (t_logits - s_logits) - ce_weight * jnp.where(hits, s_logits, 0.0)
    )
    loss_common = jnp.sum((1.0 + ce_weight) * student_log - teacher_log)

    slope_other = swapped(slope[rows:])

    terms = dot(slope[:rows], student_head, 0, 0) + dot(slope[rows:], student_other, 0, 0)
    gain_terms = jnp.sum(terms * student_rows.astype(f32), axis=0)
    gain_high, gain_low = (g.reshape(nx, 1, 1, qs) for g in high_low(gain_terms))
    loss_high, loss_low = high_low(loss_part)
    lane = lax.broadcasted_iota(jnp.int32, (nx, 1, 1, qs), 3)
    loss_row = jnp.where(lane == 0, loss_high, jnp.where(lane == 1, loss_low, 0)).astype(bf16)
    extra = jnp.concatenate([gain_high, gain_low, loss_row, jnp.zeros((nx, 1, 5, qs), bf16)], axis=2)
    extra = jnp.broadcast_to(extra, (nx, ny, 8, qs))
    sent = terms.astype(bf16).reshape(ny, held, nx, qs).transpose(2, 0, 1, 3)
    sent = jnp.concatenate([sent, extra], axis=2).reshape(nx * ny, held + 8, qs)
    got = lax.all_to_all(sent, PLANE, 0, 0, tiled=True).astype(f32).sum(axis=0)

    head_grad = (
        dot(slope[:rows], student_rows, 1, 0) + dot(slope_other, student_rows_other, 1, 0)
    ).astype(bf16)

    gain_row = got[held] + got[held + 1]
    loss_sum = got[held + 2, 0] + got[held + 2, 1]
    lane = lax.broadcasted_iota(jnp.int32, (qs,), 0)
    tail = jnp.stack([gain_row, jnp.where(lane == 0, loss_sum, 0.0)])
    tail = jnp.broadcast_to(tail[None], (nz, 2, qs))
    sent = jnp.concatenate([got[:held].reshape(nz, half, qs), tail], axis=1)
    got = lax.all_to_all(sent, Z, 0, 0, tiled=True).sum(axis=0)

    lane = lax.broadcasted_iota(jnp.int32, got.shape, 1)
    line_no = lax.broadcasted_iota(jnp.int32, got.shape, 0)
    got = jnp.where((lane == 0) & (line_no == half + 1), got + loss_common, got)
    whole = to_all(got, (X, C)).reshape(nx, nc, half + 2, qs)
    normed_grad = whole[:, :, :half].transpose(1, 2, 0, 3).reshape(own, ds)
    gain_values = student_gain.astype(f32)
    gain_grad = whole[:, :, half].sum(axis=1).reshape(ds) / gain_values
    loss = jnp.sum(whole[0, :, half + 1, 0]) / (tokens * nc)
    weighted = normed_grad * gain_values
    inner = jnp.mean(weighted * scaled, axis=1, keepdims=True)
    student_grad = inverse * (weighted - scaled * inner)
    return (loss, student_grad, gain_grad, head_grad)


def solution(mesh):
    finer = Mesh(mesh.devices.reshape(4, 2, 16, 4), SECTION_DP)
    placed = (
        P(DP, None),
        P(DP, None),
        P(),
        P(),
        P(SECTION_DP, None),
        P(SECTION_DP, None),
        P(),
        P(),
    )
    return jax.shard_map(
        on_device,
        mesh=finer,
        in_specs=placed,
        out_specs=(P(), P(DP, None), P(), P(SECTION_DP, None)),
        check_vma=False,
    )
```

```python
import jax
import jax.numpy as jnp
from jax import lax
from jax.experimental import pallas as pl
from jax.experimental.pallas import tpu as pltpu
from jax.sharding import Mesh
from jax.sharding import PartitionSpec as P

X, C, Z, Y = ("section_0", "section_1", "dp_0", "dp_1")
DP = (Z, Y)
SECTION_DP = (X, C, Z, Y)
PLANE = (X, Y)

eps = 1e-06
ce_weight = 0.5
f32 = jnp.float32
bf16 = jnp.bfloat16


def to_all(x, axes):
    length = lax.axis_size(axes)
    return lax.all_to_all(jnp.broadcast_to(x[None], (length, *x.shape)), axes, 0, 0, tiled=True)


def swapped(x):
    return lax.ppermute(x, C, [(0, 1), (1, 0)])


def shifted(x, k):
    length = lax.axis_size(X)
    return lax.ppermute(x, X, [(i, (i + k) % length) for i in range(length)])


def normalize(hidden):
    values = hidden.astype(f32)
    inverse = lax.rsqrt(jnp.mean(values * values, axis=-1, keepdims=True) + eps)
    return (values * inverse, inverse)


def merged(logs):
    peak = jnp.max(logs, axis=0)
    return peak + jnp.log(jnp.sum(jnp.exp(logs - peak[None]), axis=0))


def dot(a, b, along_a, along_b):
    return lax.dot_general(a, b, (((along_a,), (along_b,)), ((), ())), preferred_element_type=f32)


VMEM = pl.BlockSpec(memory_space=pltpu.VMEM)
SMEM = pl.BlockSpec(memory_space=pltpu.SMEM)
HBM = pl.BlockSpec(memory_space=pltpu.HBM)
MIB = 2**20


def column_log(logits):
    peak = jnp.max(logits, axis=0, keepdims=True)
    return peak + jnp.log(jnp.sum(jnp.exp(logits - peak), axis=0, keepdims=True))


def logits_kernel(
    place, a0, a1, a2, a3, b, t_own, t_other, s_own, s_other,
    t_logits, s_logits, logs, student_rows, teacher_rows, t0, t1, s0, s1, sems,
):
    copies = [
        pltpu.make_async_copy(src, dst, sems.at[k])
        for k, (src, dst) in enumerate(((t_own, t0), (t_other, t1), (s_own, s0), (s_other, s1)))
    ]
    for copy in copies:
        copy.start()
    nx = b.shape[1]
    qt = teacher_rows.shape[1] // nx
    qs = student_rows.shape[1] // nx
    half = a0.shape[0]
    for k, a in enumerate((a0, a1, a2, a3)):
        part = lax.rem(place[0] + (nx - k), nx)
        t_at = pl.ds(pl.multiple_of(part * qt, 128), qt)
        s_at = pl.ds(pl.multiple_of(part * qs, 128), qs)
        teacher_rows[0:half, t_at] = a[:, 0:qt]
        student_rows[0:half, s_at] = a[:, qt:]
        step = b.shape[2]
        for y in range(b.shape[0]):
            rows = slice(half + y * step, half + (y + 1) * step)
            teacher_rows[rows, t_at] = b[y, k, :, 0:qt]
            student_rows[rows, s_at] = b[y, k, :, qt:]
    rows = t0.shape[0]
    for k, head in enumerate((t0, t1)):
        copies[k].wait()
        total = 0.0
        for at in range(0, head.shape[1], 1024):
            total += dot(head[:, at : at + 1024], teacher_rows[:, at : at + 1024], 1, 1)
        t_logits[k * rows : (k + 1) * rows] = total
    for k, head in enumerate((s0, s1)):
        copies[2 + k].wait()
        total = 0.0
        for at in range(0, head.shape[1], 896):
            total += dot(head[:, at : at + 896], student_rows[:, at : at + 896], 1, 1)
        s_logits[k * rows : (k + 1) * rows] = total
    logs[0:1] = column_log(t_logits[...])
    logs[1:2] = column_log(s_logits[...])


def terms_kernel(
    place, got, t_logits, s_logits, label, cot, student_rows, s_own, s_other,
    slope, sent, common, s0, s1, sems,
):
    copies = [
        pltpu.make_async_copy(src, dst, sems.at[k])
        for k, (src, dst) in enumerate(((s_own, s0), (s_other, s1)))
    ]
    for copy in copies:
        copy.start()
    rows = s0.shape[0]
    nx, ny, held, _ = sent.shape
    step = held // 2
    qs = student_rows.shape[1] // nx
    half = ny * step
    teacher_log = column_log(got[:, 0, :])
    student_log = column_log(got[:, 1, :])
    common[...] = (1.0 + ce_weight) * student_log - teacher_log
    slopes = []
    loss_terms = 0.0
    for k in range(2):
        at = slice(k * rows, (k + 1) * rows)
        s_part, t_part = (s_logits[at], t_logits[at])
        entry = lax.broadcasted_iota(jnp.int32, s_part.shape, 0) + place[k]
        hits = entry == label[...]
        s_prob = jnp.exp(s_part - student_log)
        t_prob = jnp.exp(t_part - teacher_log)
        onehot = jnp.where(hits, 1.0, 0.0)
        value = cot[...] * ((1.0 + ce_weight) * s_prob - t_prob - ce_weight * onehot)
        slopes.append(value.astype(bf16))
        slope[at] = slopes[k]
        lost = t_prob * (t_part - s_part) - ce_weight * jnp.where(hits, s_part, 0.0)
        loss_terms += jnp.sum(lost, axis=0, keepdims=True)
    for copy in copies:
        copy.wait()
    line = lax.broadcasted_iota(jnp.int32, (step, 128), 0)
    loss_high = loss_terms.astype(bf16).astype(f32)
    for x in range(nx):
        at = slice(x * qs, (x + 1) * qs)
        terms = dot(slopes[0], s0[:, at], 0, 0) + dot(slopes[1], s1[:, at], 0, 0)
        gain = jnp.sum(terms * student_rows[:, at].astype(f32), axis=0, keepdims=True)
        high = gain.astype(bf16).astype(f32)
        tail = jnp.where(line == 14, loss_high, jnp.where(line == 15, loss_terms - loss_high, 0.0))
        for k in range(qs // 128):
            chunk = slice(k * 128, (k + 1) * 128)
            tail = jnp.where(line == k, high[:, chunk], tail)
            tail = jnp.where(line == 7 + k, (gain - high)[:, chunk], tail)
        terms = terms.astype(bf16)
        for y in range(ny):
            for k in range(2):
                sent[x, y, k * step : (k + 1) * step, 0:qs] = terms[
                    k * half + y * step : k * half + (y + 1) * step
                ]
            sent[x, y, 0:step, qs:] = tail.astype(bf16)
            sent[x, y, step:held, qs:] = jnp.zeros((held - step, 128), bf16)


def on_device(
    teacher_hidden,
    student_hidden,
    teacher_gain,
    student_gain,
    teacher_head,
    student_head,
    labels,
    cotangent,
):
    nx, nc, nz, ny = (lax.axis_size(a) for a in SECTION_DP)
    ix, ic, iz, iy = (lax.axis_index(a) for a in SECTION_DP)
    rows, dt = teacher_head.shape
    ds = student_head.shape[1]
    own = teacher_hidden.shape[0]
    half = own // nc
    qt, qs = (dt // nx, ds // nx)
    held = nz * half
    tokens = ny * held

    teacher_other, student_other = (swapped(teacher_head), swapped(student_head))

    t_scaled, _ = normalize(lax.dynamic_slice_in_dim(teacher_hidden, ic * half, half, 0))
    scaled, inverse = normalize(student_hidden)
    s_scaled = lax.dynamic_slice_in_dim(scaled, ic * half, half, 0)
    t_part = lax.dynamic_slice_in_dim(t_scaled, ix * qt, qt, 1)
    s_part = lax.dynamic_slice_in_dim(s_scaled, ix * qs, qs, 1)
    t_gain = lax.dynamic_slice_in_dim(teacher_gain, ix * qt, qt, 0).astype(f32)
    s_gain = lax.dynamic_slice_in_dim(student_gain, ix * qs, qs, 0).astype(f32)
    piece = jnp.concatenate(
        [(t_part * t_gain).astype(bf16), (s_part * s_gain).astype(bf16)], axis=1
    )
    line = to_all(piece, Z).reshape(held, qt + qs)

    first, second = (line[: held // 2], line[held // 2 :])
    second = jnp.stack([second] + [shifted(second, k) for k in range(1, nx)])
    first = to_all(first, Y).reshape(tokens // 2, qt + qs)
    first = [first] + [shifted(first, k) for k in range(1, nx)]
    second = to_all(second, Y)

    def of_tokens(a):
        mine = lax.dynamic_index_in_dim(a.reshape(2, nz // 2, ny, nc, half), ic, 3, keepdims=False)
        return mine.transpose(0, 2, 1, 3).reshape(1, tokens)

    def start_of(core):
        return (((ix * nc + core) * nz + iz) * ny + iy) * rows

    second, label, cot = lax.optimization_barrier((second, of_tokens(labels), of_tokens(cotangent)))

    shape = jax.ShapeDtypeStruct
    t_logits, s_logits, logs, student_rows = pl.pallas_call(
        logits_kernel,
        in_specs=[SMEM] + [VMEM] * 5 + [HBM] * 4,
        out_specs=[VMEM] * 4,
        out_shape=[
            shape((2 * rows, tokens), f32),
            shape((2 * rows, tokens), f32),
            shape((2, tokens), f32),
            shape((tokens, ds), bf16),
        ],
        scratch_shapes=[
            pltpu.VMEM((tokens, dt), bf16),
            pltpu.VMEM((rows, dt), bf16),
            pltpu.VMEM((rows, dt), bf16),
            pltpu.VMEM((rows, ds), bf16),
            pltpu.VMEM((rows, ds), bf16),
            pltpu.SemaphoreType.DMA((4,)),
        ],
        compiler_params=pltpu.CompilerParams(vmem_limit_bytes=20 * MIB),
    )(ix[None], *first, second, teacher_head, teacher_other, student_head, student_other)

    logs = merged(to_all(logs, PLANE))
    logs = to_all(logs, Z)

    slope, sent, common = pl.pallas_call(
        terms_kernel,
        in_specs=[SMEM] + [VMEM] * 6 + [HBM] * 2,
        out_specs=[VMEM] * 3,
        out_shape=[
            shape((2 * rows, tokens), bf16),
            shape((nx, ny, held, qs + 128), bf16),
            shape((1, tokens), f32),
        ],
        scratch_shapes=[
            pltpu.VMEM((rows, ds), bf16),
            pltpu.VMEM((rows, ds), bf16),
            pltpu.SemaphoreType.DMA((2,)),
        ],
        compiler_params=pltpu.CompilerParams(vmem_limit_bytes=12 * MIB),
    )(
        jnp.stack([start_of(ic), start_of(1 - ic)]),
        logs, t_logits, s_logits, label, cot, student_rows, student_head, student_other,
    )
    sent = sent.reshape(nx * ny, held, qs + 128)
    got = lax.all_to_all(sent, PLANE, 0, 0, tiled=True).astype(f32).sum(axis=0)

    student_rows, slope = lax.optimization_barrier((student_rows, slope))
    head_grad = (
        dot(slope[:rows], student_rows, 1, 0)
        + dot(swapped(slope[rows:]), swapped(student_rows), 1, 0)
    ).astype(bf16)

    tail = got[:16, qs:]
    tail = jnp.concatenate([tail[0:7] + tail[7:14], tail[14:15] + tail[15:16]]).reshape(2, 512)
    tail = jnp.broadcast_to(tail[None], (nz, half, 512))
    sent = jnp.concatenate([got[:, :qs].reshape(nz, half, qs), tail], axis=2)
    got = lax.all_to_all(sent, Z, 0, 0, tiled=True).sum(axis=0)

    whole = to_all(got, (X, C)).reshape(nx, nc, half, qs + 512)
    normed_grad = whole[:, :, :, :qs].transpose(1, 2, 0, 3).reshape(own, ds)
    tails = whole[:, :, :, qs:].sum(axis=1).reshape(nx, 8, 128)
    gain_values = student_gain.astype(f32)
    gain_grad = tails[:, :7].reshape(ds) / gain_values
    commons = common + swapped(common)
    loss = jnp.sum(tails[0, 7] + commons[0]) / (tokens * nc)
    weighted = normed_grad * gain_values
    inner = jnp.mean(weighted * scaled, axis=1, keepdims=True)
    student_grad = inverse * (weighted - scaled * inner)
    return (loss, student_grad, gain_grad, head_grad)


def solution(mesh):
    finer = Mesh(mesh.devices.reshape(4, 2, 16, 4), SECTION_DP)
    placed = (
        P(DP, None),
        P(DP, None),
        P(),
        P(),
        P(SECTION_DP, None),
        P(SECTION_DP, None),
        P(),
        P(),
    )
    return jax.shard_map(
        on_device,
        mesh=finer,
        in_specs=placed,
        out_specs=(P(), P(DP, None), P(), P(SECTION_DP, None)),
        check_vma=False,
    )
```

```python
import jax
import jax.numpy as jnp
from jax import lax
from jax.experimental import pallas as pl
from jax.experimental.pallas import tpu as pltpu
from jax.sharding import Mesh
from jax.sharding import PartitionSpec as P

X, C, Z, Y = ("section_0", "section_1", "dp_0", "dp_1")
DP = (Z, Y)
SECTION_DP = (X, C, Z, Y)
PLANE = (X, Y)

eps = 1e-06
ce_weight = 0.5
f32 = jnp.float32
bf16 = jnp.bfloat16

VMEM = pl.BlockSpec(memory_space=pltpu.VMEM)
SMEM = pl.BlockSpec(memory_space=pltpu.SMEM)
ANY = pl.BlockSpec(memory_space=pl.ANY)
MIB = 2**20
BIG = 52
shape = jax.ShapeDtypeStruct


def to_all(x, axes):
    length = lax.axis_size(axes)
    return exchanged(jnp.broadcast_to(x[None], (length, *x.shape)), axes)


def exchanged(x, axes):
    return lax.all_to_all(x, axes, 0, 0, tiled=True)


def swapped(x):
    return lax.ppermute(x, C, [(0, 1), (1, 0)])


def dot(a, b, along_a, along_b):
    return lax.dot_general(a, b, (((along_a,), (along_b,)), ((), ())), preferred_element_type=f32)


def column_log(logits):
    peak = jnp.max(logits, axis=0, keepdims=True)
    return peak + jnp.log(jnp.sum(jnp.exp(logits - peak), axis=0, keepdims=True))


def chunk(k):
    return slice(k * 128, (k + 1) * 128)


def called(kernel, in_specs, out_specs, out_shape, mib, scratch=()):
    return pl.pallas_call(
        kernel,
        in_specs=in_specs,
        out_specs=out_specs,
        out_shape=out_shape,
        scratch_shapes=list(scratch),
        compiler_params=pltpu.CompilerParams(vmem_limit_bytes=mib * MIB),
    )


def norm_kernel(
    place, teacher_at, student_at, t_gain_at, s_gain_at, out,
    teacher, student, t_gain, s_gain, t_scaled, s_scaled, gains, sems,
):
    pairs = (
        (teacher_at, teacher),
        (t_gain_at, t_gain),
        (student_at, student),
        (s_gain_at, s_gain),
    )
    copies = [pltpu.make_async_copy(a, b, sems.at[k]) for k, (a, b) in enumerate(pairs)]
    for copy in copies:
        copy.start()
    ix, ic = (place[0], place[1])
    half = out.shape[1]
    at = 0
    for n, (hidden, gain, scaled) in enumerate(
        ((teacher, t_gain, t_scaled), (student, s_gain, s_scaled))
    ):
        copies[2 * n].wait()
        copies[2 * n + 1].wait()
        values = hidden[...].astype(f32)
        inverse = lax.rsqrt(jnp.mean(values * values, axis=-1, keepdims=True) + eps)
        scaled[...] = values * inverse
        lines = gain.shape[0]
        gains[0:lines] = gain[...].astype(f32)
        width = scaled.shape[1] // 4
        part = scaled[:, pl.ds(pl.multiple_of(ix * width, 128), width)]
        mine = jnp.where(ic == 0, part[0:half], part[half : 2 * half])
        for k in range(width // 128):
            line = gains[pl.ds(ix * (width // 128) + k, 1)]
            normed = (mine[:, chunk(k)] * line).astype(bf16)
            for z in range(out.shape[0]):
                out[z, :, at : at + 128] = normed
            at += 128


def logits_kernel(
    plane, t_own, t_other, s_own, s_other,
    t_logits, s_logits, logs, student_rows,
    t_rows, s_rows, t_heads, s_heads, t_out, s_out, sems, out_sems,
):
    nx = plane.shape[0]
    qt = t_rows.shape[1] // nx
    qs = s_rows.shape[1] // nx
    rows = t_own.shape[0]
    parts = []
    for k in range(nx):
        at = slice(k * qt, (k + 1) * qt)
        parts.append(
            [
                (plane.at[k, :, 0:qt], t_rows.at[:, at]),
                (t_own.at[:, at], t_heads.at[0:rows, at]),
                (t_other.at[:, at], t_heads.at[rows:, at]),
            ]
        )
    parts.append(
        [(plane.at[k, :, qt:], s_rows.at[:, k * qs : (k + 1) * qs]) for k in range(nx)]
        + [(s_own, s_heads.at[0:rows]), (s_other, s_heads.at[rows:])]
    )
    copies, number = ([], 0)
    for part in parts:
        copies.append([])
        for source, target in part:
            copies[-1].append(pltpu.make_async_copy(source, target, sems.at[number]))
            copies[-1][-1].start()
            number += 1
    total = 0.0
    for k in range(nx):
        for copy in copies[k]:
            copy.wait()
        at = slice(k * qt, (k + 1) * qt)
        total += dot(t_heads[:, at], t_rows[:, at], 1, 1)
    t_out[...] = total
    back = [pltpu.make_async_copy(t_out, t_logits, out_sems.at[0])]
    back[0].start()
    for copy in copies[nx]:
        copy.wait()
    back.append(pltpu.make_async_copy(s_rows, student_rows, out_sems.at[1]))
    back[1].start()
    s_out[...] = dot(s_heads[...], s_rows[...], 1, 1)
    back.append(pltpu.make_async_copy(s_out, s_logits, out_sems.at[2]))
    back[2].start()
    t_log = column_log(t_out[...])
    s_log = column_log(s_out[...])
    for k in range(logs.shape[0]):
        logs[k, 0:1] = t_log
        logs[k, 1:2] = s_log
    for copy in back:
        copy.wait()


def merge_kernel(got, out):
    t_log = column_log(got[:, 0, :])
    s_log = column_log(got[:, 1, :])
    for k in range(out.shape[0]):
        out[k, 0:1] = t_log
        out[k, 1:2] = s_log


def terms_kernel(
    place, got, label, cot, t_logits, s_logits, student_rows, s_own, s_other,
    slope, sent, common, t_in, s_in, s_rows, s_heads, sems,
):
    rows = s_own.shape[0]
    pairs = (
        (t_logits, t_in),
        (s_logits, s_in),
        (s_own, s_heads.at[0:rows]),
        (s_other, s_heads.at[rows:]),
        (student_rows, s_rows),
    )
    copies = [pltpu.make_async_copy(a, b, sems.at[k]) for k, (a, b) in enumerate(pairs)]
    for copy in copies:
        copy.start()
    nx, ny, held, _ = sent.shape
    qs = s_rows.shape[1] // nx
    teacher_log = column_log(got[:, 0, :])
    student_log = column_log(got[:, 1, :])
    common[...] = (1.0 + ce_weight) * student_log - teacher_log
    loss_terms = 0.0
    copies[0].wait()
    copies[1].wait()
    for k in range(2):
        at = slice(k * rows, (k + 1) * rows)
        s_part, t_part = (s_in[at], t_in[at])
        entry = lax.broadcasted_iota(jnp.int32, s_part.shape, 0) + place[2 + k]
        hits = entry == label[...]
        s_prob = jnp.exp(s_part - student_log)
        t_prob = jnp.exp(t_part - teacher_log)
        onehot = jnp.where(hits, 1.0, 0.0)
        value = cot[...] * ((1.0 + ce_weight) * s_prob - t_prob - ce_weight * onehot)
        slope[at] = value.astype(bf16)
        lost = t_prob * (t_part - s_part) - ce_weight * jnp.where(hits, s_part, 0.0)
        loss_terms += jnp.sum(lost, axis=0, keepdims=True)
    for copy in copies[2:]:
        copy.wait()
    line = lax.broadcasted_iota(jnp.int32, (16, 128), 0)
    loss_high = loss_terms.astype(bf16).astype(f32)
    slopes = slope[...]
    for x in range(nx):
        at = slice(x * qs, (x + 1) * qs)
        terms = dot(slopes, s_heads[:, at], 0, 0)
        gain = jnp.sum(terms * s_rows[:, at].astype(f32), axis=0, keepdims=True)
        high = gain.astype(bf16).astype(f32)
        tail = jnp.where(line == 14, loss_high, jnp.where(line == 15, loss_terms - loss_high, 0.0))
        for k in range(qs // 128):
            tail = jnp.where(line == k, high[:, chunk(k)], tail)
            tail = jnp.where(line == 7 + k, (gain - high)[:, chunk(k)], tail)
        terms = terms.astype(bf16)
        for y in range(ny):
            sent[x, y, :, 0:qs] = terms[y * held : (y + 1) * held]
            sent[x, y, 0:16, qs:] = tail.astype(bf16)
            sent[x, y, 16:held, qs:] = jnp.zeros((held - 16, 128), bf16)


def repack_kernel(got, out):
    total = got[0].astype(f32)
    for k in range(1, got.shape[0]):
        total += got[k].astype(f32)
    nz, half, _ = out.shape
    qs = got.shape[2] - 128
    tail = total[0:16, qs:]
    lines = [tail[k : k + 1] + tail[7 + k : 8 + k] for k in range(7)]
    lines.append(tail[14:15] + tail[15:16])
    pairs = [jnp.concatenate([lines[k], lines[4 + k]], axis=0) for k in range(4)]
    for z in range(nz):
        out[z, :, 0:qs] = total[z * half : (z + 1) * half, 0:qs]
        for k in range(4):
            out[z, :, qs + k * 128 : qs + (k + 1) * 128] = pairs[k]


def share_kernel(got, common, out):
    total = got[0]
    for k in range(1, got.shape[0]):
        total += got[k]
    width = out.shape[2] - 128
    for k in range(out.shape[0]):
        out[k] = total
        out[k, 1:2, width:] = total[1:2, width:] + common[...]


def final_kernel(got, hidden, gain, student_grad, gain_grad, loss, gains):
    values = hidden[...].astype(f32)
    own, ds = values.shape
    inverse = lax.rsqrt(jnp.mean(values * values, axis=-1, keepdims=True) + eps)
    scaled = values * inverse
    gains[...] = gain[...].astype(f32)
    each = gain.shape[0] // 4
    qs = each * 128
    inner = 0.0
    weighted = []
    for x in range(4):
        pair = (got[2 * x], got[2 * x + 1])
        for k in range(each):
            line = x * each + k
            grad = jnp.concatenate([p[:, chunk(k)] for p in pair], axis=0)
            weighted.append(grad * gains[line : line + 1])
            inner += jnp.sum(weighted[-1] * scaled[:, chunk(line)], axis=1, keepdims=True)
            row, at = (k // 4, qs + (k % 4) * 128)
            both = sum(p[row : row + 1, at : at + 128] for p in pair)
            gain_grad[line : line + 1] = both / gains[line : line + 1]
    inner = inner * (1.0 / ds)
    for k in range(4 * each):
        student_grad[:, chunk(k)] = inverse * (weighted[k] - scaled[:, chunk(k)] * inner)
    at = qs + 384
    lost = got[0][1:2, at:] + got[1][1:2, at:]
    loss[...] = jnp.sum(lost, axis=1, keepdims=True) * (1.0 / 256)


def on_device(
    teacher_hidden,
    student_hidden,
    teacher_gain,
    student_gain,
    teacher_head,
    student_head,
    labels,
    cotangent,
):
    nx, nc, nz, ny = (lax.axis_size(a) for a in SECTION_DP)
    ix, ic, iz, iy = (lax.axis_index(a) for a in SECTION_DP)
    rows, dt = teacher_head.shape
    own, ds = student_hidden.shape
    half = own // nc
    qt, qs = (dt // nx, ds // nx)
    held = nz * half
    tokens = ny * held

    def start_of(core):
        return (((ix * nc + core) * nz + iz) * ny + iy) * rows

    place = jnp.stack([ix, ic, start_of(ic), start_of(1 - ic)])
    t_gain, s_gain = (g.reshape(-1, 128) for g in (teacher_gain, student_gain))
    pieces = called(
        norm_kernel,
        [SMEM] + [ANY] * 4,
        VMEM,
        shape((nz, half, qt + qs), bf16),
        BIG,
        [
            pltpu.VMEM((own, dt), bf16),
            pltpu.VMEM((own, ds), bf16),
            pltpu.VMEM((dt // 128, 128), bf16),
            pltpu.VMEM((ds // 128, 128), bf16),
            pltpu.VMEM((own, dt), f32),
            pltpu.VMEM((own, ds), f32),
            pltpu.VMEM((dt // 128, 128), f32),
            pltpu.SemaphoreType.DMA((4,)),
        ],
    )(place, teacher_hidden, student_hidden, t_gain, s_gain)

    pieces, teacher_head, student_head = lax.optimization_barrier(
        (pieces, teacher_head, student_head)
    )
    teacher_other, student_other = (swapped(teacher_head), swapped(student_head))

    def of_tokens(a):
        mine = lax.dynamic_index_in_dim(a.reshape(nz, ny, nc, half), ic, 2, keepdims=False)
        return mine.transpose(1, 0, 2).reshape(1, tokens)

    line = exchanged(pieces, Z).reshape(held, qt + qs)
    line, teacher_other, student_other, label, cot = lax.optimization_barrier(
        (line, teacher_other, student_other, of_tokens(labels), of_tokens(cotangent))
    )
    plane = to_all(line, PLANE).reshape(nx, tokens, qt + qs)

    t_logits, s_logits, logs, student_rows = called(
        logits_kernel,
        [ANY] * 5,
        [ANY, ANY, VMEM, ANY],
        [
            shape((2 * rows, tokens), f32),
            shape((2 * rows, tokens), f32),
            shape((nx * ny, 2, tokens), f32),
            shape((tokens, ds), bf16),
        ],
        BIG,
        [
            pltpu.VMEM((tokens, dt), bf16),
            pltpu.VMEM((tokens, ds), bf16),
            pltpu.VMEM((2 * rows, dt), bf16),
            pltpu.VMEM((2 * rows, ds), bf16),
            pltpu.VMEM((2 * rows, tokens), f32),
            pltpu.VMEM((2 * rows, tokens), f32),
            pltpu.SemaphoreType.DMA((4 * nx + 2,)),
            pltpu.SemaphoreType.DMA((3,)),
        ],
    )(plane, teacher_head, teacher_other, student_head, student_other)
    logs = exchanged(logs, PLANE)
    logs = called(merge_kernel, [VMEM], VMEM, shape((nz, 2, tokens), f32), 4)(logs)
    logs = exchanged(logs, Z)

    slope, sent, common = called(
        terms_kernel,
        [SMEM] + [VMEM] * 3 + [ANY] * 5,
        [VMEM] * 3,
        [
            shape((2 * rows, tokens), bf16),
            shape((nx, ny, held, qs + 128), bf16),
            shape((1, tokens), f32),
        ],
        BIG,
        [
            pltpu.VMEM((2 * rows, tokens), f32),
            pltpu.VMEM((2 * rows, tokens), f32),
            pltpu.VMEM((tokens, ds), bf16),
            pltpu.VMEM((2 * rows, ds), bf16),
            pltpu.SemaphoreType.DMA((5,)),
        ],
    )(place, logs, label, cot, t_logits, s_logits, student_rows, student_head, student_other)
    got = exchanged(sent.reshape(nx * ny, held, qs + 128), PLANE)
    got, student_rows, slope = lax.optimization_barrier((got, student_rows, slope))
    got = called(repack_kernel, [VMEM], VMEM, shape((nz, half, qs + 512), f32), 8)(got)
    got = exchanged(got, Z)

    head_grad = (
        dot(slope[:rows], student_rows, 1, 0)
        + dot(swapped(slope[rows:]), swapped(student_rows), 1, 0)
    ).astype(bf16)

    got = called(share_kernel, [VMEM] * 2, VMEM, shape((nx * nc, half, qs + 512), f32), 4)(
        got, common
    )
    got, head_grad = lax.optimization_barrier((exchanged(got, (X, C)), head_grad))
    student_grad, gain_grad, loss = called(
        final_kernel,
        [VMEM] * 3,
        [VMEM] * 3,
        [shape((own, ds), f32), shape((ds // 128, 128), f32), shape((1, 1), f32)],
        4,
        [pltpu.VMEM((ds // 128, 128), f32)],
    )(got, student_hidden, s_gain)
    return (loss.reshape(()), student_grad, gain_grad.reshape(ds), head_grad)


def solution(mesh):
    finer = Mesh(mesh.devices.reshape(4, 2, 16, 4), SECTION_DP)
    placed = (
        P(DP, None),
        P(DP, None),
        P(),
        P(),
        P(SECTION_DP, None),
        P(SECTION_DP, None),
        P(),
        P(),
    )
    return jax.shard_map(
        on_device,
        mesh=finer,
        in_specs=placed,
        out_specs=(P(), P(DP, None), P(), P(SECTION_DP, None)),
        check_vma=False,
    )
```

```python
import jax
import jax.numpy as jnp
from jax import lax
from jax.experimental import pallas as pl
from jax.experimental.pallas import tpu as pltpu
from jax.sharding import Mesh
from jax.sharding import PartitionSpec as P

X, C, Z, Y = ("section_0", "section_1", "dp_0", "dp_1")
DP = (Z, Y)
SECTION_DP = (X, C, Z, Y)
PLANE = (X, Y)

eps = 1e-06
ce_weight = 0.5
f32 = jnp.float32
bf16 = jnp.bfloat16

VMEM = pl.BlockSpec(memory_space=pltpu.VMEM)
SMEM = pl.BlockSpec(memory_space=pltpu.SMEM)
ANY = pl.BlockSpec(memory_space=pl.ANY)
MIB = 2**20
NORM = 8
LOGITS = 8
BIG = 16
shape = jax.ShapeDtypeStruct


def to_all(x, axes):
    length = lax.axis_size(axes)
    return exchanged(jnp.broadcast_to(x[None], (length, *x.shape)), axes)


def exchanged(x, axes):
    return lax.all_to_all(x, axes, 0, 0, tiled=True)


def swapped(x):
    return lax.ppermute(x, C, [(0, 1), (1, 0)])


def dot(a, b, along_a, along_b):
    return lax.dot_general(a, b, (((along_a,), (along_b,)), ((), ())), preferred_element_type=f32)


def column_log(logits):
    peak = jnp.max(logits, axis=0, keepdims=True)
    return peak + jnp.log(jnp.sum(jnp.exp(logits - peak), axis=0, keepdims=True))


def chunk(k):
    return slice(k * 128, (k + 1) * 128)


def called(kernel, in_specs, out_specs, out_shape, mib, scratch=()):
    return pl.pallas_call(
        kernel,
        in_specs=in_specs,
        out_specs=out_specs,
        out_shape=out_shape,
        scratch_shapes=list(scratch),
        compiler_params=pltpu.CompilerParams(vmem_limit_bytes=mib * MIB),
    )


def norm_kernel(
    place, teacher_at, student_at, t_gain_at, s_gain_at, out,
    teacher, student, t_gain, s_gain, t_scaled, s_scaled, gains, sems,
):
    pairs = (
        (teacher_at, teacher),
        (t_gain_at, t_gain),
        (student_at, student),
        (s_gain_at, s_gain),
    )
    copies = [pltpu.make_async_copy(a, b, sems.at[k]) for k, (a, b) in enumerate(pairs)]
    for copy in copies:
        copy.start()
    ix, ic = (place[0], place[1])
    half = out.shape[1]
    at = 0
    for n, (hidden, gain, scaled) in enumerate(
        ((teacher, t_gain, t_scaled), (student, s_gain, s_scaled))
    ):
        copies[2 * n].wait()
        copies[2 * n + 1].wait()
        values = hidden[...].astype(f32)
        inverse = lax.rsqrt(jnp.mean(values * values, axis=-1, keepdims=True) + eps)
        scaled[...] = values * inverse
        lines = gain.shape[0]
        gains[0:lines] = gain[...].astype(f32)
        width = scaled.shape[1] // 4
        part = scaled[:, pl.ds(pl.multiple_of(ix * width, 128), width)]
        mine = jnp.where(ic == 0, part[0:half], part[half : 2 * half])
        for k in range(width // 128):
            line = gains[pl.ds(ix * (width // 128) + k, 1)]
            normed = (mine[:, chunk(k)] * line).astype(bf16)
            for z in range(out.shape[0]):
                out[z, :, at : at + 128] = normed
            at += 128


def logits_kernel(
    plane, t_heads, s_heads, t_logits, s_logits, logs, student_rows, t_out, s_out, sems
):
    nx = plane.shape[0]
    nc, rows, dt = t_heads.shape
    qt = dt // nx
    qs = s_heads.shape[2] // nx
    back = [
        pltpu.make_async_copy(
            plane.at[k, :, qt:], student_rows.at[:, k * qs : (k + 1) * qs], sems.at[k]
        )
        for k in range(nx)
    ]
    back.append(pltpu.make_async_copy(t_out, t_logits, sems.at[nx]))
    back.append(pltpu.make_async_copy(s_out, s_logits, sems.at[nx + 1]))
    for copy in back[:nx]:
        copy.start()
    for n in range(nc):
        total = 0.0
        for k in range(nx):
            total += dot(t_heads[n, :, k * qt : (k + 1) * qt], plane[k, :, 0:qt], 1, 1)
        t_out[n * rows : (n + 1) * rows] = total
    back[nx].start()
    for n in range(nc):
        total = 0.0
        for k in range(nx):
            total += dot(s_heads[n, :, k * qs : (k + 1) * qs], plane[k, :, qt:], 1, 1)
        s_out[n * rows : (n + 1) * rows] = total
    back[nx + 1].start()
    t_log = column_log(t_out[...])
    s_log = column_log(s_out[...])
    for k in range(logs.shape[0]):
        logs[k, 0:1] = t_log
        logs[k, 1:2] = s_log
    for copy in back:
        copy.wait()


def merge_kernel(got, out):
    t_log = column_log(got[:, 0, :])
    s_log = column_log(got[:, 1, :])
    for k in range(out.shape[0]):
        out[k, 0:1] = t_log
        out[k, 1:2] = s_log


def terms_kernel(
    place, got, label, cot, t_logits, s_logits, student_rows, s_heads_at,
    slope, sent, common, t_in, s_in, s_rows, s_heads, sems,
):
    rows = s_heads_at.shape[1]
    pairs = (
        (t_logits, t_in),
        (s_logits, s_in),
        (s_heads_at, s_heads),
        (student_rows, s_rows),
    )
    copies = [pltpu.make_async_copy(a, b, sems.at[k]) for k, (a, b) in enumerate(pairs)]
    for copy in copies:
        copy.start()
    nx, ny, held, _ = sent.shape
    qs = s_rows.shape[1] // nx
    teacher_log = column_log(got[:, 0, :])
    student_log = column_log(got[:, 1, :])
    common[...] = (1.0 + ce_weight) * student_log - teacher_log
    loss_terms = 0.0
    copies[0].wait()
    copies[1].wait()
    for k in range(2):
        at = slice(k * rows, (k + 1) * rows)
        s_part, t_part = (s_in[at], t_in[at])
        entry = lax.broadcasted_iota(jnp.int32, s_part.shape, 0) + place[2 + k]
        hits = entry == label[...]
        s_prob = jnp.exp(s_part - student_log)
        t_prob = jnp.exp(t_part - teacher_log)
        onehot = jnp.where(hits, 1.0, 0.0)
        value = cot[...] * ((1.0 + ce_weight) * s_prob - t_prob - ce_weight * onehot)
        slope[at] = value.astype(bf16)
        lost = t_prob * (t_part - s_part) - ce_weight * jnp.where(hits, s_part, 0.0)
        loss_terms += jnp.sum(lost, axis=0, keepdims=True)
    for copy in copies[2:]:
        copy.wait()
    line = lax.broadcasted_iota(jnp.int32, (16, 128), 0)
    loss_high = loss_terms.astype(bf16).astype(f32)
    slopes = slope[...]
    for x in range(nx):
        at = slice(x * qs, (x + 1) * qs)
        terms = dot(slopes[:rows], s_heads[0, :, at], 0, 0)
        terms += dot(slopes[rows:], s_heads[1, :, at], 0, 0)
        gain = jnp.sum(terms * s_rows[:, at].astype(f32), axis=0, keepdims=True)
        high = gain.astype(bf16).astype(f32)
        tail = jnp.where(line == 14, loss_high, jnp.where(line == 15, loss_terms - loss_high, 0.0))
        for k in range(qs // 128):
            tail = jnp.where(line == k, high[:, chunk(k)], tail)
            tail = jnp.where(line == 7 + k, (gain - high)[:, chunk(k)], tail)
        terms = terms.astype(bf16)
        for y in range(ny):
            sent[x, y, :, 0:qs] = terms[y * held : (y + 1) * held]
            sent[x, y, 0:16, qs:] = tail.astype(bf16)
            sent[x, y, 16:held, qs:] = jnp.zeros((held - 16, 128), bf16)


def repack_kernel(got, out):
    total = got[0].astype(f32)
    for k in range(1, got.shape[0]):
        total += got[k].astype(f32)
    nz, half, _ = out.shape
    qs = got.shape[2] - 128
    tail = total[0:16, qs:]
    lines = [tail[k : k + 1] + tail[7 + k : 8 + k] for k in range(7)]
    lines.append(tail[14:15] + tail[15:16])
    pairs = [jnp.concatenate([lines[k], lines[4 + k]], axis=0) for k in range(4)]
    for z in range(nz):
        out[z, :, 0:qs] = total[z * half : (z + 1) * half, 0:qs]
        for k in range(4):
            out[z, :, qs + k * 128 : qs + (k + 1) * 128] = pairs[k]


def share_kernel(got, common, out):
    total = got[0]
    for k in range(1, got.shape[0]):
        total += got[k]
    width = out.shape[2] - 128
    for k in range(out.shape[0]):
        out[k] = total
        out[k, 1:2, width:] = total[1:2, width:] + common[...]


def final_kernel(got, hidden, gain, student_grad, gain_grad, loss, gains):
    values = hidden[...].astype(f32)
    own, ds = values.shape
    inverse = lax.rsqrt(jnp.mean(values * values, axis=-1, keepdims=True) + eps)
    scaled = values * inverse
    gains[...] = gain[...].astype(f32)
    each = gain.shape[0] // 4
    qs = each * 128
    inner = 0.0
    weighted = []
    for x in range(4):
        pair = (got[2 * x], got[2 * x + 1])
        for k in range(each):
            line = x * each + k
            grad = jnp.concatenate([p[:, chunk(k)] for p in pair], axis=0)
            weighted.append(grad * gains[line : line + 1])
            inner += jnp.sum(weighted[-1] * scaled[:, chunk(line)], axis=1, keepdims=True)
            row, at = (k // 4, qs + (k % 4) * 128)
            both = sum(p[row : row + 1, at : at + 128] for p in pair)
            gain_grad[line : line + 1] = both / gains[line : line + 1]
    inner = inner * (1.0 / ds)
    for k in range(4 * each):
        student_grad[:, chunk(k)] = inverse * (weighted[k] - scaled[:, chunk(k)] * inner)
    at = qs + 384
    lost = got[0][1:2, at:] + got[1][1:2, at:]
    loss[...] = jnp.sum(lost, axis=1, keepdims=True) * (1.0 / 256)


def on_device(
    teacher_hidden,
    student_hidden,
    teacher_gain,
    student_gain,
    teacher_head,
    student_head,
    labels,
    cotangent,
):
    nx, nc, nz, ny = (lax.axis_size(a) for a in SECTION_DP)
    ix, ic, iz, iy = (lax.axis_index(a) for a in SECTION_DP)
    rows, dt = teacher_head.shape
    own, ds = student_hidden.shape
    half = own // nc
    qt, qs = (dt // nx, ds // nx)
    held = nz * half
    tokens = ny * held

    def start_of(core):
        return (((ix * nc + core) * nz + iz) * ny + iy) * rows

    place = jnp.stack([ix, ic, start_of(0), start_of(1)])
    t_gain, s_gain = (g.reshape(-1, 128) for g in (teacher_gain, student_gain))
    pieces = called(
        norm_kernel,
        [SMEM] + [ANY] * 4,
        VMEM,
        shape((nz, half, qt + qs), bf16),
        NORM,
        [
            pltpu.VMEM((own, dt), bf16),
            pltpu.VMEM((own, ds), bf16),
            pltpu.VMEM((dt // 128, 128), bf16),
            pltpu.VMEM((ds // 128, 128), bf16),
            pltpu.VMEM((own, dt), f32),
            pltpu.VMEM((own, ds), f32),
            pltpu.VMEM((dt // 128, 128), f32),
            pltpu.SemaphoreType.DMA((4,)),
        ],
    )(place, teacher_hidden, student_hidden, t_gain, s_gain)

    def of_tokens(a):
        mine = lax.dynamic_index_in_dim(a.reshape(nz, ny, nc, half), ic, 2, keepdims=False)
        return mine.transpose(1, 0, 2).reshape(1, tokens)

    pieces, labels, cotangent = lax.optimization_barrier((pieces, labels, cotangent))
    label, cot = (of_tokens(labels), of_tokens(cotangent))
    t_heads, s_heads = (lax.all_gather(a, C) for a in (teacher_head, student_head))

    line = exchanged(pieces, Z).reshape(held, qt + qs)
    line, label, cot, t_heads, s_heads = lax.optimization_barrier(
        (line, label, cot, t_heads, s_heads)
    )
    plane = to_all(line, PLANE).reshape(nx, tokens, qt + qs)

    t_logits, s_logits, logs, student_rows = called(
        logits_kernel,
        [VMEM] * 3,
        [ANY, ANY, VMEM, ANY],
        [
            shape((2 * rows, tokens), f32),
            shape((2 * rows, tokens), f32),
            shape((nx * ny, 2, tokens), f32),
            shape((tokens, ds), bf16),
        ],
        LOGITS,
        [
            pltpu.VMEM((2 * rows, tokens), f32),
            pltpu.VMEM((2 * rows, tokens), f32),
            pltpu.SemaphoreType.DMA((nx + 2,)),
        ],
    )(plane, t_heads, s_heads)
    logs = exchanged(logs, PLANE)
    logs = called(merge_kernel, [VMEM], VMEM, shape((nz, 2, tokens), f32), 4)(logs)
    logs = exchanged(logs, Z)

    slope, sent, common = called(
        terms_kernel,
        [SMEM] + [VMEM] * 3 + [ANY] * 4,
        [VMEM] * 3,
        [
            shape((2 * rows, tokens), bf16),
            shape((nx, ny, held, qs + 128), bf16),
            shape((1, tokens), f32),
        ],
        BIG,
        [
            pltpu.VMEM((2 * rows, tokens), f32),
            pltpu.VMEM((2 * rows, tokens), f32),
            pltpu.VMEM((tokens, ds), bf16),
            pltpu.VMEM((nc, rows, ds), bf16),
            pltpu.SemaphoreType.DMA((4,)),
        ],
    )(place, logs, label, cot, t_logits, s_logits, student_rows, s_heads)
    got = exchanged(sent.reshape(nx * ny, held, qs + 128), PLANE)
    got = called(repack_kernel, [VMEM], VMEM, shape((nz, half, qs + 512), f32), 8)(got)
    got, student_rows, slope = lax.optimization_barrier((got, student_rows, slope))
    got = exchanged(got, Z)

    mine = lax.dynamic_slice_in_dim(slope, ic * rows, rows, 0)
    others = lax.dynamic_slice_in_dim(slope, (1 - ic) * rows, rows, 0)
    head_grad = (
        dot(mine, student_rows, 1, 0) + dot(swapped(others), swapped(student_rows), 1, 0)
    ).astype(bf16)

    got = called(share_kernel, [VMEM] * 2, VMEM, shape((nx * nc, half, qs + 512), f32), 4)(
        got, common
    )
    got, head_grad = lax.optimization_barrier((exchanged(got, (X, C)), head_grad))
    student_grad, gain_grad, loss = called(
        final_kernel,
        [VMEM] * 3,
        [VMEM] * 3,
        [shape((own, ds), f32), shape((ds // 128, 128), f32), shape((1, 1), f32)],
        4,
        [pltpu.VMEM((ds // 128, 128), f32)],
    )(got, student_hidden, s_gain)
    return (loss.reshape(()), student_grad, gain_grad.reshape(ds), head_grad)


def solution(mesh):
    finer = Mesh(mesh.devices.reshape(4, 2, 16, 4), SECTION_DP)
    placed = (
        P(DP, None),
        P(DP, None),
        P(),
        P(),
        P(SECTION_DP, None),
        P(SECTION_DP, None),
        P(),
        P(),
    )
    return jax.shard_map(
        on_device,
        mesh=finer,
        in_specs=placed,
        out_specs=(P(), P(DP, None), P(), P(SECTION_DP, None)),
        check_vma=False,
    )
```

```python
import jax
import jax.numpy as jnp
from jax import lax
from jax.experimental import pallas as pl
from jax.experimental.pallas import tpu as pltpu
from jax.sharding import Mesh
from jax.sharding import PartitionSpec as P

X, C, Z, Y = ("section_0", "section_1", "dp_0", "dp_1")
DP = (Z, Y)
SECTION_DP = (X, C, Z, Y)
PLANE = (X, Y)

eps = 1e-06
ce_weight = 0.5
f32 = jnp.float32
bf16 = jnp.bfloat16

VMEM = pl.BlockSpec(memory_space=pltpu.VMEM)
SMEM = pl.BlockSpec(memory_space=pltpu.SMEM)
ANY = pl.BlockSpec(memory_space=pl.ANY)
MIB = 2**20
NORM = 63
LOGITS = 8
BIG = 16
shape = jax.ShapeDtypeStruct


def to_all(x, axes):
    length = lax.axis_size(axes)
    return exchanged(jnp.broadcast_to(x[None], (length, *x.shape)), axes)


def exchanged(x, axes):
    return lax.all_to_all(x, axes, 0, 0, tiled=True)


def swapped(x):
    return lax.ppermute(x, C, [(0, 1), (1, 0)])


def dot(a, b, along_a, along_b):
    return lax.dot_general(a, b, (((along_a,), (along_b,)), ((), ())), preferred_element_type=f32)


def column_log(logits):
    peak = jnp.max(logits, axis=0, keepdims=True)
    return peak + jnp.log(jnp.sum(jnp.exp(logits - peak), axis=0, keepdims=True))


def chunk(k):
    return slice(k * 128, (k + 1) * 128)


def called(kernel, in_specs, out_specs, out_shape, mib, scratch=()):
    return pl.pallas_call(
        kernel,
        in_specs=in_specs,
        out_specs=out_specs,
        out_shape=out_shape,
        scratch_shapes=list(scratch),
        compiler_params=pltpu.CompilerParams(vmem_limit_bytes=mib * MIB),
    )


def norm_kernel(
    place, teacher_at, student_at, t_gain_at, s_gain_at, out,
    teacher, student, t_gain, s_gain, t_scaled, s_scaled, gains, sems,
):
    pairs = (
        (teacher_at, teacher),
        (t_gain_at, t_gain),
        (student_at, student),
        (s_gain_at, s_gain),
    )
    copies = [pltpu.make_async_copy(a, b, sems.at[k]) for k, (a, b) in enumerate(pairs)]
    for copy in copies:
        copy.start()
    ix, ic = (place[0], place[1])
    half = out.shape[1]
    at = 0
    for n, (hidden, gain, scaled) in enumerate(
        ((teacher, t_gain, t_scaled), (student, s_gain, s_scaled))
    ):
        copies[2 * n].wait()
        copies[2 * n + 1].wait()
        values = hidden[...].astype(f32)
        inverse = lax.rsqrt(jnp.mean(values * values, axis=-1, keepdims=True) + eps)
        scaled[...] = values * inverse
        lines = gain.shape[0]
        gains[0:lines] = gain[...].astype(f32)
        width = scaled.shape[1] // 4
        part = scaled[:, pl.ds(pl.multiple_of(ix * width, 128), width)]
        mine = jnp.where(ic == 0, part[0:half], part[half : 2 * half])
        for k in range(width // 128):
            line = gains[pl.ds(ix * (width // 128) + k, 1)]
            normed = (mine[:, chunk(k)] * line).astype(bf16)
            for z in range(out.shape[0]):
                out[z, :, at : at + 128] = normed
            at += 128


def logits_kernel(
    plane, t_own, t_other, s_own, s_other, t_logits, s_logits, logs, student_rows, t_out, s_out, sems
):
    nx = plane.shape[0]
    rows, dt = t_own.shape
    qt = dt // nx
    qs = s_own.shape[1] // nx
    back = [
        pltpu.make_async_copy(
            plane.at[k, :, qt:], student_rows.at[:, k * qs : (k + 1) * qs], sems.at[k]
        )
        for k in range(nx)
    ]
    back.append(pltpu.make_async_copy(t_out, t_logits, sems.at[nx]))
    back.append(pltpu.make_async_copy(s_out, s_logits, sems.at[nx + 1]))
    for copy in back[:nx]:
        copy.start()
    for n, head in enumerate((t_own, t_other)):
        total = 0.0
        for k in range(nx):
            total += dot(head[:, k * qt : (k + 1) * qt], plane[k, :, 0:qt], 1, 1)
        t_out[n * rows : (n + 1) * rows] = total
    back[nx].start()
    for n, head in enumerate((s_own, s_other)):
        total = 0.0
        for k in range(nx):
            total += dot(head[:, k * qs : (k + 1) * qs], plane[k, :, qt:], 1, 1)
        s_out[n * rows : (n + 1) * rows] = total
    back[nx + 1].start()
    t_log = column_log(t_out[...])
    s_log = column_log(s_out[...])
    for k in range(logs.shape[0]):
        logs[k, 0:1] = t_log
        logs[k, 1:2] = s_log
    for copy in back:
        copy.wait()


def merge_kernel(got, out):
    t_log = column_log(got[:, 0, :])
    s_log = column_log(got[:, 1, :])
    for k in range(out.shape[0]):
        out[k, 0:1] = t_log
        out[k, 1:2] = s_log


def terms_kernel(
    place, got, label, cot, t_logits, s_logits, student_rows, s_own, s_other,
    slope, sent, common, t_in, s_in, s_rows, s_heads, sems,
):
    rows = s_own.shape[0]
    pairs = (
        (t_logits, t_in),
        (s_logits, s_in),
        (s_own, s_heads.at[0]),
        (s_other, s_heads.at[1]),
        (student_rows, s_rows),
    )
    copies = [pltpu.make_async_copy(a, b, sems.at[k]) for k, (a, b) in enumerate(pairs)]
    for copy in copies:
        copy.start()
    nx, ny, held, _ = sent.shape
    qs = s_rows.shape[1] // nx
    teacher_log = column_log(got[:, 0, :])
    student_log = column_log(got[:, 1, :])
    common[...] = (1.0 + ce_weight) * student_log - teacher_log
    loss_terms = 0.0
    copies[0].wait()
    copies[1].wait()
    for k in range(2):
        at = slice(k * rows, (k + 1) * rows)
        s_part, t_part = (s_in[at], t_in[at])
        entry = lax.broadcasted_iota(jnp.int32, s_part.shape, 0) + place[2 + k]
        hits = entry == label[...]
        s_prob = jnp.exp(s_part - student_log)
        t_prob = jnp.exp(t_part - teacher_log)
        onehot = jnp.where(hits, 1.0, 0.0)
        value = cot[...] * ((1.0 + ce_weight) * s_prob - t_prob - ce_weight * onehot)
        slope[at] = value.astype(bf16)
        lost = t_prob * (t_part - s_part) - ce_weight * jnp.where(hits, s_part, 0.0)
        loss_terms += jnp.sum(lost, axis=0, keepdims=True)
    for copy in copies[2:]:
        copy.wait()
    line = lax.broadcasted_iota(jnp.int32, (16, 128), 0)
    loss_high = loss_terms.astype(bf16).astype(f32)
    slopes = slope[...]
    for x in range(nx):
        at = slice(x * qs, (x + 1) * qs)
        terms = dot(slopes[:rows], s_heads[0, :, at], 0, 0)
        terms += dot(slopes[rows:], s_heads[1, :, at], 0, 0)
        gain = jnp.sum(terms * s_rows[:, at].astype(f32), axis=0, keepdims=True)
        high = gain.astype(bf16).astype(f32)
        tail = jnp.where(line == 14, loss_high, jnp.where(line == 15, loss_terms - loss_high, 0.0))
        for k in range(qs // 128):
            tail = jnp.where(line == k, high[:, chunk(k)], tail)
            tail = jnp.where(line == 7 + k, (gain - high)[:, chunk(k)], tail)
        terms = terms.astype(bf16)
        for y in range(ny):
            sent[x, y, :, 0:qs] = terms[y * held : (y + 1) * held]
            sent[x, y, 0:16, qs:] = tail.astype(bf16)
            sent[x, y, 16:held, qs:] = jnp.zeros((held - 16, 128), bf16)


def repack_kernel(got, out):
    total = got[0].astype(f32)
    for k in range(1, got.shape[0]):
        total += got[k].astype(f32)
    nz, half, _ = out.shape
    qs = got.shape[2] - 128
    tail = total[0:16, qs:]
    lines = [tail[k : k + 1] + tail[7 + k : 8 + k] for k in range(7)]
    lines.append(tail[14:15] + tail[15:16])
    pairs = [jnp.concatenate([lines[k], lines[4 + k]], axis=0) for k in range(4)]
    for z in range(nz):
        out[z, :, 0:qs] = total[z * half : (z + 1) * half, 0:qs]
        for k in range(4):
            out[z, :, qs + k * 128 : qs + (k + 1) * 128] = pairs[k]


def share_kernel(got, common, out):
    total = got[0]
    for k in range(1, got.shape[0]):
        total += got[k]
    width = out.shape[2] - 128
    for k in range(out.shape[0]):
        out[k] = total
        out[k, 1:2, width:] = total[1:2, width:] + common[...]


def final_kernel(got, hidden, gain, student_grad, gain_grad, loss, gains):
    values = hidden[...].astype(f32)
    own, ds = values.shape
    inverse = lax.rsqrt(jnp.mean(values * values, axis=-1, keepdims=True) + eps)
    scaled = values * inverse
    gains[...] = gain[...].astype(f32)
    each = gain.shape[0] // 4
    qs = each * 128
    inner = 0.0
    weighted = []
    for x in range(4):
        pair = (got[2 * x], got[2 * x + 1])
        for k in range(each):
            line = x * each + k
            grad = jnp.concatenate([p[:, chunk(k)] for p in pair], axis=0)
            weighted.append(grad * gains[line : line + 1])
            inner += jnp.sum(weighted[-1] * scaled[:, chunk(line)], axis=1, keepdims=True)
            row, at = (k // 4, qs + (k % 4) * 128)
            both = sum(p[row : row + 1, at : at + 128] for p in pair)
            gain_grad[line : line + 1] = both / gains[line : line + 1]
    inner = inner * (1.0 / ds)
    for k in range(4 * each):
        student_grad[:, chunk(k)] = inverse * (weighted[k] - scaled[:, chunk(k)] * inner)
    at = qs + 384
    lost = got[0][1:2, at:] + got[1][1:2, at:]
    loss[...] = jnp.sum(lost, axis=1, keepdims=True) * (1.0 / 256)


def on_device(
    teacher_hidden,
    student_hidden,
    teacher_gain,
    student_gain,
    teacher_head,
    student_head,
    labels,
    cotangent,
):
    nx, nc, nz, ny = (lax.axis_size(a) for a in SECTION_DP)
    ix, ic, iz, iy = (lax.axis_index(a) for a in SECTION_DP)
    rows, dt = teacher_head.shape
    own, ds = student_hidden.shape
    half = own // nc
    qt, qs = (dt // nx, ds // nx)
    held = nz * half
    tokens = ny * held

    def start_of(core):
        return (((ix * nc + core) * nz + iz) * ny + iy) * rows

    place = jnp.stack([ix, ic, start_of(ic), start_of(1 - ic)])
    t_gain, s_gain = (g.reshape(-1, 128) for g in (teacher_gain, student_gain))
    pieces = called(
        norm_kernel,
        [SMEM] + [ANY] * 4,
        VMEM,
        shape((nz, half, qt + qs), bf16),
        NORM,
        [
            pltpu.VMEM((own, dt), bf16),
            pltpu.VMEM((own, ds), bf16),
            pltpu.VMEM((dt // 128, 128), bf16),
            pltpu.VMEM((ds // 128, 128), bf16),
            pltpu.VMEM((own, dt), f32),
            pltpu.VMEM((own, ds), f32),
            pltpu.VMEM((dt // 128, 128), f32),
            pltpu.SemaphoreType.DMA((4,)),
        ],
    )(place, teacher_hidden, student_hidden, t_gain, s_gain)

    def of_tokens(a):
        mine = lax.dynamic_index_in_dim(a.reshape(nz, ny, nc, half), ic, 2, keepdims=False)
        return mine.transpose(1, 0, 2).reshape(1, tokens)

    pieces, labels, cotangent = lax.optimization_barrier((pieces, labels, cotangent))
    label, cot = (of_tokens(labels), of_tokens(cotangent))
    pieces, teacher_head, student_head = lax.optimization_barrier(
        (pieces, teacher_head, student_head)
    )
    teacher_other, student_other = (swapped(teacher_head), swapped(student_head))

    line = exchanged(pieces, Z).reshape(held, qt + qs)
    line, label, cot, teacher_other, student_other = lax.optimization_barrier(
        (line, label, cot, teacher_other, student_other)
    )
    plane = to_all(line, PLANE).reshape(nx, tokens, qt + qs)

    t_logits, s_logits, logs, student_rows = called(
        logits_kernel,
        [VMEM] * 5,
        [ANY, ANY, VMEM, ANY],
        [
            shape((2 * rows, tokens), f32),
            shape((2 * rows, tokens), f32),
            shape((nx * ny, 2, tokens), f32),
            shape((tokens, ds), bf16),
        ],
        LOGITS,
        [
            pltpu.VMEM((2 * rows, tokens), f32),
            pltpu.VMEM((2 * rows, tokens), f32),
            pltpu.SemaphoreType.DMA((nx + 2,)),
        ],
    )(plane, teacher_head, teacher_other, student_head, student_other)
    logs = exchanged(logs, PLANE)
    logs = called(merge_kernel, [VMEM], VMEM, shape((nz, 2, tokens), f32), 4)(logs)
    logs = exchanged(logs, Z)

    slope, sent, common = called(
        terms_kernel,
        [SMEM] + [VMEM] * 3 + [ANY] * 5,
        [VMEM] * 3,
        [
            shape((2 * rows, tokens), bf16),
            shape((nx, ny, held, qs + 128), bf16),
            shape((1, tokens), f32),
        ],
        BIG,
        [
            pltpu.VMEM((2 * rows, tokens), f32),
            pltpu.VMEM((2 * rows, tokens), f32),
            pltpu.VMEM((tokens, ds), bf16),
            pltpu.VMEM((nc, rows, ds), bf16),
            pltpu.SemaphoreType.DMA((5,)),
        ],
    )(place, logs, label, cot, t_logits, s_logits, student_rows, student_head, student_other)
    got = exchanged(sent.reshape(nx * ny, held, qs + 128), PLANE)
    got = called(repack_kernel, [VMEM], VMEM, shape((nz, half, qs + 512), f32), 8)(got)
    got, slope = lax.optimization_barrier((got, slope))
    got = exchanged(got, Z)
    slope_other, student_rows = lax.optimization_barrier((slope[rows:], student_rows))

    head_grad = (
        dot(slope[:rows], student_rows, 1, 0)
        + dot(swapped(slope_other), swapped(student_rows), 1, 0)
    ).astype(bf16)

    got = called(share_kernel, [VMEM] * 2, VMEM, shape((nx * nc, half, qs + 512), f32), 4)(
        got, common
    )
    got, head_grad = lax.optimization_barrier((exchanged(got, (X, C)), head_grad))
    student_grad, gain_grad, loss = called(
        final_kernel,
        [VMEM] * 3,
        [VMEM] * 3,
        [shape((own, ds), f32), shape((ds // 128, 128), f32), shape((1, 1), f32)],
        4,
        [pltpu.VMEM((ds // 128, 128), f32)],
    )(got, student_hidden, s_gain)
    return (loss.reshape(()), student_grad, gain_grad.reshape(ds), head_grad)


def solution(mesh):
    finer = Mesh(mesh.devices.reshape(4, 2, 16, 4), SECTION_DP)
    placed = (
        P(DP, None),
        P(DP, None),
        P(),
        P(),
        P(SECTION_DP, None),
        P(SECTION_DP, None),
        P(),
        P(),
    )
    return jax.shard_map(
        on_device,
        mesh=finer,
        in_specs=placed,
        out_specs=(P(), P(DP, None), P(), P(SECTION_DP, None)),
        check_vma=False,
    )
```

```python
import jax
import jax.numpy as jnp
from jax import lax
from jax.experimental import pallas as pl
from jax.experimental.pallas import tpu as pltpu
from jax.sharding import Mesh
from jax.sharding import PartitionSpec as P

X, C, Z, Y = ("section_0", "section_1", "dp_0", "dp_1")
DP = (Z, Y)
SECTION_DP = (X, C, Z, Y)
PLANE = (X, Y)

eps = 1e-06
ce_weight = 0.5
f32 = jnp.float32
bf16 = jnp.bfloat16

VMEM = pl.BlockSpec(memory_space=pltpu.VMEM)
SMEM = pl.BlockSpec(memory_space=pltpu.SMEM)
ANY = pl.BlockSpec(memory_space=pl.ANY)
MIB = 2**20
NORM = 63
LOGITS = 10
BIG = 16
shape = jax.ShapeDtypeStruct


def to_all(x, axes):
    length = lax.axis_size(axes)
    return exchanged(jnp.broadcast_to(x[None], (length, *x.shape)), axes)


def exchanged(x, axes):
    return lax.all_to_all(x, axes, 0, 0, tiled=True)


def swapped(x):
    return lax.ppermute(x, C, [(0, 1), (1, 0)])


def dot(a, b, along_a, along_b):
    return lax.dot_general(a, b, (((along_a,), (along_b,)), ((), ())), preferred_element_type=f32)


def column_log(logits):
    peak = jnp.max(logits, axis=0, keepdims=True)
    return peak + jnp.log(jnp.sum(jnp.exp(logits - peak), axis=0, keepdims=True))


def chunk(k):
    return slice(k * 128, (k + 1) * 128)


def called(kernel, in_specs, out_specs, out_shape, mib, scratch=()):
    return pl.pallas_call(
        kernel,
        in_specs=in_specs,
        out_specs=out_specs,
        out_shape=out_shape,
        scratch_shapes=list(scratch),
        compiler_params=pltpu.CompilerParams(vmem_limit_bytes=mib * MIB),
    )


def norm_kernel(
    at_x, at_c, teacher_at, student_at, t_gain_at, s_gain_at, out,
    teacher, student, t_gain, s_gain, t_scaled, s_scaled, gains, sems,
):
    pairs = (
        (teacher_at, teacher),
        (t_gain_at, t_gain),
        (student_at, student),
        (s_gain_at, s_gain),
    )
    copies = [pltpu.make_async_copy(a, b, sems.at[k]) for k, (a, b) in enumerate(pairs)]
    for copy in copies:
        copy.start()
    ix, ic = (at_x[0], at_c[0])
    half = out.shape[1]
    at = 0
    for n, (hidden, gain, scaled) in enumerate(
        ((teacher, t_gain, t_scaled), (student, s_gain, s_scaled))
    ):
        copies[2 * n].wait()
        copies[2 * n + 1].wait()
        values = hidden[...].astype(f32)
        inverse = lax.rsqrt(jnp.mean(values * values, axis=-1, keepdims=True) + eps)
        scaled[...] = values * inverse
        lines = gain.shape[0]
        gains[0:lines] = gain[...].astype(f32)
        width = scaled.shape[1] // 4
        part = scaled[:, pl.ds(pl.multiple_of(ix * width, 128), width)]
        mine = jnp.where(ic == 0, part[0:half], part[half : 2 * half])
        for k in range(width // 128):
            line = gains[pl.ds(ix * (width // 128) + k, 1)]
            normed = (mine[:, chunk(k)] * line).astype(bf16)
            for z in range(out.shape[0]):
                out[z, :, at : at + 128] = normed
            at += 128


def logits_kernel(
    plane, t_own, s_own, s_other, t_other_at, t_logits, s_logits, logs, student_rows,
    t_other, t_out, s_out, sems,
):
    nx = plane.shape[0]
    rows, dt = t_own.shape
    qt = dt // nx
    qs = s_own.shape[1] // nx
    late = pltpu.make_async_copy(t_other_at, t_other, sems.at[nx + 2])
    late.start()
    back = [
        pltpu.make_async_copy(
            plane.at[k, :, qt:], student_rows.at[:, k * qs : (k + 1) * qs], sems.at[k]
        )
        for k in range(nx)
    ]
    back.append(pltpu.make_async_copy(t_out, t_logits, sems.at[nx]))
    back.append(pltpu.make_async_copy(s_out, s_logits, sems.at[nx + 1]))
    for copy in back[:nx]:
        copy.start()
    for out, n, head, at, width in (
        (s_out, 0, s_own, qt, qs),
        (s_out, 1, s_other, qt, qs),
        (t_out, 0, t_own, 0, qt),
        (t_out, 1, t_other, 0, qt),
    ):
        if head is t_other:
            back[nx + 1].start()
            late.wait()
        total = 0.0
        for k in range(nx):
            part = plane[k, :, at : at + width]
            total += dot(head[:, k * width : (k + 1) * width], part, 1, 1)
        out[n * rows : (n + 1) * rows] = total
    back[nx].start()
    t_log = column_log(t_out[...])
    s_log = column_log(s_out[...])
    for k in range(logs.shape[0]):
        logs[k, 0:1] = t_log
        logs[k, 1:2] = s_log
    for copy in back:
        copy.wait()


def merge_kernel(got, out):
    t_log = column_log(got[:, 0, :])
    s_log = column_log(got[:, 1, :])
    for k in range(out.shape[0]):
        out[k, 0:1] = t_log
        out[k, 1:2] = s_log


def terms_kernel(
    place, got, label, cot, t_logits, s_logits, student_rows, s_own, s_other,
    slope, sent, common, t_in, s_in, s_rows, s_heads, sems,
):
    rows = s_own.shape[0]
    pairs = (
        (t_logits, t_in),
        (s_logits, s_in),
        (s_own, s_heads.at[0]),
        (s_other, s_heads.at[1]),
        (student_rows, s_rows),
    )
    copies = [pltpu.make_async_copy(a, b, sems.at[k]) for k, (a, b) in enumerate(pairs)]
    for copy in copies:
        copy.start()
    nx, ny, held, _ = sent.shape
    qs = s_rows.shape[1] // nx
    teacher_log = column_log(got[:, 0, :])
    student_log = column_log(got[:, 1, :])
    common[...] = (1.0 + ce_weight) * student_log - teacher_log
    loss_terms = 0.0
    copies[0].wait()
    copies[1].wait()
    for k in range(2):
        at = slice(k * rows, (k + 1) * rows)
        s_part, t_part = (s_in[at], t_in[at])
        entry = lax.broadcasted_iota(jnp.int32, s_part.shape, 0) + place[k]
        hits = entry == label[...]
        s_prob = jnp.exp(s_part - student_log)
        t_prob = jnp.exp(t_part - teacher_log)
        onehot = jnp.where(hits, 1.0, 0.0)
        value = cot[...] * ((1.0 + ce_weight) * s_prob - t_prob - ce_weight * onehot)
        slope[at] = value.astype(bf16)
        lost = t_prob * (t_part - s_part) - ce_weight * jnp.where(hits, s_part, 0.0)
        loss_terms += jnp.sum(lost, axis=0, keepdims=True)
    for copy in copies[2:]:
        copy.wait()
    line = lax.broadcasted_iota(jnp.int32, (16, 128), 0)
    loss_high = loss_terms.astype(bf16).astype(f32)
    slopes = slope[...]
    for x in range(nx):
        at = slice(x * qs, (x + 1) * qs)
        terms = dot(slopes[:rows], s_heads[0, :, at], 0, 0)
        terms += dot(slopes[rows:], s_heads[1, :, at], 0, 0)
        gain = jnp.sum(terms * s_rows[:, at].astype(f32), axis=0, keepdims=True)
        high = gain.astype(bf16).astype(f32)
        tail = jnp.where(line == 14, loss_high, jnp.where(line == 15, loss_terms - loss_high, 0.0))
        for k in range(qs // 128):
            tail = jnp.where(line == k, high[:, chunk(k)], tail)
            tail = jnp.where(line == 7 + k, (gain - high)[:, chunk(k)], tail)
        terms = terms.astype(bf16)
        for y in range(ny):
            sent[x, y, :, 0:qs] = terms[y * held : (y + 1) * held]
            sent[x, y, 0:16, qs:] = tail.astype(bf16)
            sent[x, y, 16:held, qs:] = jnp.zeros((held - 16, 128), bf16)


def repack_kernel(got, out):
    total = got[0].astype(f32)
    for k in range(1, got.shape[0]):
        total += got[k].astype(f32)
    nz, half, _ = out.shape
    qs = got.shape[2] - 128
    tail = total[0:16, qs:]
    lines = [tail[k : k + 1] + tail[7 + k : 8 + k] for k in range(7)]
    lines.append(tail[14:15] + tail[15:16])
    pairs = []
    for line in lines:
        high = line.astype(bf16).astype(f32)
        pairs.append(jnp.concatenate([high, line - high], axis=0).astype(bf16))
    for z in range(nz):
        out[z, :, 0:qs] = total[z * half : (z + 1) * half, 0:qs].astype(bf16)
        for k in range(8):
            out[z, :, qs + k * 128 : qs + (k + 1) * 128] = pairs[k]


def share_kernel(got, common, out):
    total = got[0].astype(f32)
    for k in range(1, got.shape[0]):
        total += got[k].astype(f32)
    qs = out.shape[2] - 512
    lines = [total[0:1, qs + k * 128 : qs + (k + 1) * 128] for k in range(8)]
    lines = [x + total[1:2, qs + k * 128 : qs + (k + 1) * 128] for k, x in enumerate(lines)]
    lines[7] += common[...]
    for k in range(out.shape[0]):
        out[k, :, 0:qs] = total[:, 0:qs]
        for n in range(8):
            at = qs + (n % 4) * 128
            out[k, n // 4 : n // 4 + 1, at : at + 128] = lines[n]


def final_kernel(got, hidden, gain, student_grad, gain_grad, loss, gains):
    values = hidden[...].astype(f32)
    own, ds = values.shape
    inverse = lax.rsqrt(jnp.mean(values * values, axis=-1, keepdims=True) + eps)
    scaled = values * inverse
    gains[...] = gain[...].astype(f32)
    each = gain.shape[0] // 4
    qs = each * 128
    inner = 0.0
    weighted = []
    for x in range(4):
        pair = (got[2 * x], got[2 * x + 1])
        for k in range(each):
            line = x * each + k
            grad = jnp.concatenate([p[:, chunk(k)] for p in pair], axis=0)
            weighted.append(grad * gains[line : line + 1])
            inner += jnp.sum(weighted[-1] * scaled[:, chunk(line)], axis=1, keepdims=True)
            row, at = (k // 4, qs + (k % 4) * 128)
            both = sum(p[row : row + 1, at : at + 128] for p in pair)
            gain_grad[line : line + 1] = both / gains[line : line + 1]
    inner = inner * (1.0 / ds)
    for k in range(4 * each):
        student_grad[:, chunk(k)] = inverse * (weighted[k] - scaled[:, chunk(k)] * inner)
    at = qs + 384
    lost = got[0][1:2, at:] + got[1][1:2, at:]
    loss[...] = jnp.sum(lost, axis=1, keepdims=True) * (1.0 / 256)


def on_device(
    teacher_hidden,
    student_hidden,
    teacher_gain,
    student_gain,
    teacher_head,
    student_head,
    labels,
    cotangent,
):
    nx, nc, nz, ny = (lax.axis_size(a) for a in SECTION_DP)
    ix, ic, iz, iy = (lax.axis_index(a) for a in SECTION_DP)
    rows, dt = teacher_head.shape
    own, ds = student_hidden.shape
    half = own // nc
    qt, qs = (dt // nx, ds // nx)
    held = nz * half
    tokens = ny * held

    def start_of(core):
        return (((ix * nc + core) * nz + iz) * ny + iy) * rows

    t_gain, s_gain = (g.reshape(-1, 128) for g in (teacher_gain, student_gain))
    pieces = called(
        norm_kernel,
        [SMEM] * 2 + [ANY] * 4,
        VMEM,
        shape((nz, half, qt + qs), bf16),
        NORM,
        [
            pltpu.VMEM((own, dt), bf16),
            pltpu.VMEM((own, ds), bf16),
            pltpu.VMEM((dt // 128, 128), bf16),
            pltpu.VMEM((ds // 128, 128), bf16),
            pltpu.VMEM((own, dt), f32),
            pltpu.VMEM((own, ds), f32),
            pltpu.VMEM((dt // 128, 128), f32),
            pltpu.SemaphoreType.DMA((4,)),
        ],
    )(ix[None], ic[None], teacher_hidden, student_hidden, t_gain, s_gain)

    def of_tokens(a):
        mine = lax.dynamic_index_in_dim(a.reshape(nz, ny, nc, half), ic, 2, keepdims=False)
        return mine.transpose(1, 0, 2).reshape(1, tokens)

    pieces, labels, cotangent, ix = lax.optimization_barrier((pieces, labels, cotangent, ix))
    label, cot = (of_tokens(labels), of_tokens(cotangent))
    pieces, teacher_head, student_head = lax.optimization_barrier(
        (pieces, teacher_head, student_head)
    )
    teacher_other, student_other = (swapped(teacher_head), swapped(student_head))

    line = exchanged(pieces, Z).reshape(held, qt + qs)
    place = jnp.stack([start_of(ic), start_of(1 - ic)])
    line, place, label, cot, teacher_other, student_other = lax.optimization_barrier(
        (line, place, label, cot, teacher_other, student_other)
    )
    plane = to_all(line, PLANE).reshape(nx, tokens, qt + qs)

    t_logits, s_logits, logs, student_rows = called(
        logits_kernel,
        [VMEM] * 4 + [ANY],
        [ANY, ANY, VMEM, ANY],
        [
            shape((2 * rows, tokens), f32),
            shape((2 * rows, tokens), f32),
            shape((nx * ny, 2, tokens), f32),
            shape((tokens, ds), bf16),
        ],
        LOGITS,
        [
            pltpu.VMEM((rows, dt), bf16),
            pltpu.VMEM((2 * rows, tokens), f32),
            pltpu.VMEM((2 * rows, tokens), f32),
            pltpu.SemaphoreType.DMA((nx + 3,)),
        ],
    )(plane, teacher_head, student_head, student_other, teacher_other)
    logs = exchanged(logs, PLANE)
    logs = called(merge_kernel, [VMEM], VMEM, shape((nz, 2, tokens), f32), 4)(logs)
    logs = exchanged(logs, Z)

    slope, sent, common = called(
        terms_kernel,
        [SMEM] + [VMEM] * 3 + [ANY] * 5,
        [VMEM] * 3,
        [
            shape((2 * rows, tokens), bf16),
            shape((nx, ny, held, qs + 128), bf16),
            shape((1, tokens), f32),
        ],
        BIG,
        [
            pltpu.VMEM((2 * rows, tokens), f32),
            pltpu.VMEM((2 * rows, tokens), f32),
            pltpu.VMEM((tokens, ds), bf16),
            pltpu.VMEM((nc, rows, ds), bf16),
            pltpu.SemaphoreType.DMA((5,)),
        ],
    )(place, logs, label, cot, t_logits, s_logits, student_rows, student_head, student_other)
    got = exchanged(sent.reshape(nx * ny, held, qs + 128), PLANE)
    got = called(repack_kernel, [VMEM], VMEM, shape((nz, half, qs + 1024), bf16), 8)(got)
    got, slope = lax.optimization_barrier((got, slope))
    got = exchanged(got, Z)
    slope_other, student_rows = lax.optimization_barrier((slope[rows:], student_rows))

    head_grad = (
        dot(slope[:rows], student_rows, 1, 0)
        + dot(swapped(slope_other), swapped(student_rows), 1, 0)
    ).astype(bf16)

    got = called(share_kernel, [VMEM] * 2, VMEM, shape((nx * nc, half, qs + 512), f32), 4)(
        got, common
    )
    got, head_grad = lax.optimization_barrier((exchanged(got, (X, C)), head_grad))
    student_grad, gain_grad, loss = called(
        final_kernel,
        [VMEM] * 3,
        [VMEM] * 3,
        [shape((own, ds), f32), shape((ds // 128, 128), f32), shape((1, 1), f32)],
        4,
        [pltpu.VMEM((ds // 128, 128), f32)],
    )(got, student_hidden, s_gain)
    return (loss.reshape(()), student_grad, gain_grad.reshape(ds), head_grad)


def solution(mesh):
    finer = Mesh(mesh.devices.reshape(4, 2, 16, 4), SECTION_DP)
    placed = (
        P(DP, None),
        P(DP, None),
        P(),
        P(),
        P(SECTION_DP, None),
        P(SECTION_DP, None),
        P(),
        P(),
    )
    return jax.shard_map(
        on_device,
        mesh=finer,
        in_specs=placed,
        out_specs=(P(), P(DP, None), P(), P(SECTION_DP, None)),
        check_vma=False,
    )
```

```python
import jax
import jax.numpy as jnp
from jax import lax
from jax.experimental import pallas as pl
from jax.experimental.pallas import tpu as pltpu
from jax.sharding import Mesh
from jax.sharding import PartitionSpec as P

X, C, Z, Y = ("section_0", "section_1", "dp_0", "dp_1")
DP = (Z, Y)
SECTION_DP = (X, C, Z, Y)
PLANE = (X, Y)

eps = 1e-06
ce_weight = 0.5
f32 = jnp.float32
bf16 = jnp.bfloat16

VMEM = pl.BlockSpec(memory_space=pltpu.VMEM)
SMEM = pl.BlockSpec(memory_space=pltpu.SMEM)
ANY = pl.BlockSpec(memory_space=pl.ANY)
MIB = 2**20
NORM = 63
LOGITS = 10
BIG = 16
shape = jax.ShapeDtypeStruct


def to_all(x, axes):
    length = lax.axis_size(axes)
    return exchanged(jnp.broadcast_to(x[None], (length, *x.shape)), axes)


def exchanged(x, axes):
    return lax.all_to_all(x, axes, 0, 0, tiled=True)


def swapped(x):
    return lax.ppermute(x, C, [(0, 1), (1, 0)])


def dot(a, b, along_a, along_b):
    return lax.dot_general(a, b, (((along_a,), (along_b,)), ((), ())), preferred_element_type=f32)


def column_log(logits):
    peak = jnp.max(logits, axis=0, keepdims=True)
    return peak + jnp.log(jnp.sum(jnp.exp(logits - peak), axis=0, keepdims=True))


def chunk(k):
    return slice(k * 128, (k + 1) * 128)


def called(kernel, in_specs, out_specs, out_shape, mib, scratch=()):
    return pl.pallas_call(
        kernel,
        in_specs=in_specs,
        out_specs=out_specs,
        out_shape=out_shape,
        scratch_shapes=list(scratch),
        compiler_params=pltpu.CompilerParams(vmem_limit_bytes=mib * MIB),
    )


def norm_kernel(
    at_x, at_c, teacher_at, student_at, t_gain_at, s_gain_at, out,
    teacher, student, t_gain, s_gain, t_scaled, s_scaled, gains, sems,
):
    pairs = (
        (teacher_at, teacher),
        (t_gain_at, t_gain),
        (student_at, student),
        (s_gain_at, s_gain),
    )
    copies = [pltpu.make_async_copy(a, b, sems.at[k]) for k, (a, b) in enumerate(pairs)]
    for copy in copies:
        copy.start()
    ix, ic = (at_x[0], at_c[0])
    half = out.shape[1]
    at = 0
    for n, (hidden, gain, scaled) in enumerate(
        ((teacher, t_gain, t_scaled), (student, s_gain, s_scaled))
    ):
        copies[2 * n].wait()
        copies[2 * n + 1].wait()
        values = hidden[...].astype(f32)
        inverse = lax.rsqrt(jnp.mean(values * values, axis=-1, keepdims=True) + eps)
        scaled[...] = values * inverse
        lines = gain.shape[0]
        gains[0:lines] = gain[...].astype(f32)
        width = scaled.shape[1] // 4
        part = scaled[:, pl.ds(pl.multiple_of(ix * width, 128), width)]
        mine = jnp.where(ic == 0, part[0:half], part[half : 2 * half])
        for k in range(width // 128):
            line = gains[pl.ds(ix * (width // 128) + k, 1)]
            normed = (mine[:, chunk(k)] * line).astype(bf16)
            for z in range(out.shape[0]):
                out[z, :, at : at + 128] = normed
            at += 128


def logits_kernel(
    plane, t_own, s_own, s_other, t_other_at,
    t_logits, s_logits, logs, student_rows, early_rows, late_rows, t_other, sems,
):
    nx, tokens, _ = plane.shape
    rows, dt = t_own.shape
    qt = dt // nx
    qs = s_own.shape[1] // nx
    late = pltpu.make_async_copy(t_other_at, t_other, sems.at[0])
    late.start()
    back = []
    for k in range(nx):
        at = slice(k * qs, (k + 1) * qs)
        for n, (target, first, last) in enumerate(
            (
                (student_rows, 0, tokens),
                (early_rows, 0, tokens // 2),
                (late_rows, tokens // 2, tokens),
            )
        ):
            back.append(
                pltpu.make_async_copy(
                    plane.at[k, first:last, qt:], target.at[:, at], sems.at[1 + 3 * k + n]
                )
            )
            back[-1].start()
    for out, n, head, at, width in (
        (s_logits, 0, s_own, qt, qs),
        (s_logits, 1, s_other, qt, qs),
        (t_logits, 0, t_own, 0, qt),
        (t_logits, 1, t_other, 0, qt),
    ):
        if head is t_other:
            late.wait()
        total = 0.0
        for k in range(nx):
            part = plane[k, :, at : at + width]
            total += dot(head[:, k * width : (k + 1) * width], part, 1, 1)
        out[n * rows : (n + 1) * rows] = total
    t_log = column_log(t_logits[...])
    s_log = column_log(s_logits[...])
    for k in range(logs.shape[0]):
        logs[k, 0:1] = t_log
        logs[k, 1:2] = s_log
    for copy in back:
        copy.wait()


def merge_kernel(got, out):
    t_log = column_log(got[:, 0, :])
    s_log = column_log(got[:, 1, :])
    for k in range(out.shape[0]):
        out[k, 0:1] = t_log
        out[k, 1:2] = s_log


def terms_kernel(
    place, got, label, cot, t_logits, s_logits, s_rows_at, s_own, s_other,
    slope, sent, common, s_rows, s_heads, sems,
):
    rows = s_own.shape[0]
    pairs = ((s_own, s_heads.at[0]), (s_other, s_heads.at[1]), (s_rows_at, s_rows))
    copies = [pltpu.make_async_copy(a, b, sems.at[k]) for k, (a, b) in enumerate(pairs)]
    for copy in copies:
        copy.start()
    nx, ny, held, _ = sent.shape
    qs = s_rows.shape[1] // nx
    teacher_log = column_log(got[:, 0, :])
    student_log = column_log(got[:, 1, :])
    common[...] = (1.0 + ce_weight) * student_log - teacher_log
    loss_terms = 0.0
    for k in range(2):
        at = slice(k * rows, (k + 1) * rows)
        s_part, t_part = (s_logits[at], t_logits[at])
        entry = lax.broadcasted_iota(jnp.int32, s_part.shape, 0) + place[k]
        hits = entry == label[...]
        s_prob = jnp.exp(s_part - student_log)
        t_prob = jnp.exp(t_part - teacher_log)
        onehot = jnp.where(hits, 1.0, 0.0)
        value = cot[...] * ((1.0 + ce_weight) * s_prob - t_prob - ce_weight * onehot)
        slope[at] = value.astype(bf16)
        lost = t_prob * (t_part - s_part) - ce_weight * jnp.where(hits, s_part, 0.0)
        loss_terms += jnp.sum(lost, axis=0, keepdims=True)
    for copy in copies:
        copy.wait()
    line = lax.broadcasted_iota(jnp.int32, (16, 128), 0)
    loss_high = loss_terms.astype(bf16).astype(f32)
    slopes = slope[...]
    for x in range(nx):
        at = slice(x * qs, (x + 1) * qs)
        terms = dot(slopes[:rows], s_heads[0, :, at], 0, 0)
        terms += dot(slopes[rows:], s_heads[1, :, at], 0, 0)
        gain = jnp.sum(terms * s_rows[:, at].astype(f32), axis=0, keepdims=True)
        high = gain.astype(bf16).astype(f32)
        tail = jnp.where(line == 14, loss_high, jnp.where(line == 15, loss_terms - loss_high, 0.0))
        for k in range(qs // 128):
            tail = jnp.where(line == k, high[:, chunk(k)], tail)
            tail = jnp.where(line == 7 + k, (gain - high)[:, chunk(k)], tail)
        terms = terms.astype(bf16)
        for y in range(ny):
            sent[x, y, :, 0:qs] = terms[y * held : (y + 1) * held]
            sent[x, y, 0:16, qs:] = tail.astype(bf16)
            sent[x, y, 16:held, qs:] = jnp.zeros((held - 16, 128), bf16)


def repack_kernel(got, out):
    total = got[0].astype(f32)
    for k in range(1, got.shape[0]):
        total += got[k].astype(f32)
    nz, half, _ = out.shape
    qs = got.shape[2] - 128
    tail = total[0:16, qs:]
    lines = [tail[k : k + 1] + tail[7 + k : 8 + k] for k in range(7)]
    lines.append(tail[14:15] + tail[15:16])
    pairs = []
    for line in lines:
        high = line.astype(bf16).astype(f32)
        pairs.append(jnp.concatenate([high, line - high], axis=0).astype(bf16))
    for z in range(nz):
        out[z, :, 0:qs] = total[z * half : (z + 1) * half, 0:qs].astype(bf16)
        for k in range(8):
            out[z, :, qs + k * 128 : qs + (k + 1) * 128] = pairs[k]


def share_kernel(got, common, out):
    total = got[0].astype(f32)
    for k in range(1, got.shape[0]):
        total += got[k].astype(f32)
    qs = out.shape[2] - 512
    lines = [total[0:1, qs + k * 128 : qs + (k + 1) * 128] for k in range(8)]
    lines = [x + total[1:2, qs + k * 128 : qs + (k + 1) * 128] for k, x in enumerate(lines)]
    lines[7] += common[...]
    for k in range(out.shape[0]):
        out[k, :, 0:qs] = total[:, 0:qs]
        for n in range(8):
            at = qs + (n % 4) * 128
            out[k, n // 4 : n // 4 + 1, at : at + 128] = lines[n]


def final_kernel(got, hidden, gain, student_grad, gain_grad, loss, gains):
    values = hidden[...].astype(f32)
    own, ds = values.shape
    inverse = lax.rsqrt(jnp.mean(values * values, axis=-1, keepdims=True) + eps)
    scaled = values * inverse
    gains[...] = gain[...].astype(f32)
    each = gain.shape[0] // 4
    qs = each * 128
    inner = 0.0
    weighted = []
    for x in range(4):
        pair = (got[2 * x], got[2 * x + 1])
        for k in range(each):
            line = x * each + k
            grad = jnp.concatenate([p[:, chunk(k)] for p in pair], axis=0)
            weighted.append(grad * gains[line : line + 1])
            inner += jnp.sum(weighted[-1] * scaled[:, chunk(line)], axis=1, keepdims=True)
            row, at = (k // 4, qs + (k % 4) * 128)
            both = sum(p[row : row + 1, at : at + 128] for p in pair)
            gain_grad[line : line + 1] = both / gains[line : line + 1]
    inner = inner * (1.0 / ds)
    for k in range(4 * each):
        student_grad[:, chunk(k)] = inverse * (weighted[k] - scaled[:, chunk(k)] * inner)
    at = qs + 384
    lost = got[0][1:2, at:] + got[1][1:2, at:]
    loss[...] = jnp.sum(lost, axis=1, keepdims=True) * (1.0 / 256)


def on_device(
    teacher_hidden,
    student_hidden,
    teacher_gain,
    student_gain,
    teacher_head,
    student_head,
    labels,
    cotangent,
):
    nx, nc, nz, ny = (lax.axis_size(a) for a in SECTION_DP)
    ix, ic, iz, iy = (lax.axis_index(a) for a in SECTION_DP)
    rows, dt = teacher_head.shape
    own, ds = student_hidden.shape
    half = own // nc
    qt, qs = (dt // nx, ds // nx)
    held = nz * half
    tokens = ny * held

    def start_of(core):
        return (((ix * nc + core) * nz + iz) * ny + iy) * rows

    t_gain, s_gain = (g.reshape(-1, 128) for g in (teacher_gain, student_gain))
    pieces = called(
        norm_kernel,
        [SMEM] * 2 + [ANY] * 4,
        VMEM,
        shape((nz, half, qt + qs), bf16),
        NORM,
        [
            pltpu.VMEM((own, dt), bf16),
            pltpu.VMEM((own, ds), bf16),
            pltpu.VMEM((dt // 128, 128), bf16),
            pltpu.VMEM((ds // 128, 128), bf16),
            pltpu.VMEM((own, dt), f32),
            pltpu.VMEM((own, ds), f32),
            pltpu.VMEM((dt // 128, 128), f32),
            pltpu.SemaphoreType.DMA((4,)),
        ],
    )(ix[None], ic[None], teacher_hidden, student_hidden, t_gain, s_gain)

    def of_tokens(a):
        mine = lax.dynamic_index_in_dim(a.reshape(nz, ny, nc, half), ic, 2, keepdims=False)
        return mine.transpose(1, 0, 2).reshape(1, tokens)

    pieces, labels, cotangent, ix = lax.optimization_barrier((pieces, labels, cotangent, ix))
    label, cot = (of_tokens(labels), of_tokens(cotangent))
    pieces, teacher_head, student_head = lax.optimization_barrier(
        (pieces, teacher_head, student_head)
    )
    teacher_other, student_other = (swapped(teacher_head), swapped(student_head))

    line = exchanged(pieces, Z).reshape(held, qt + qs)
    place = jnp.stack([start_of(ic), start_of(1 - ic)])
    line, place, label, cot, teacher_other, student_other = lax.optimization_barrier(
        (line, place, label, cot, teacher_other, student_other)
    )
    plane = to_all(line, PLANE).reshape(nx, tokens, qt + qs)

    t_logits, s_logits, logs, student_rows, early_rows, late_rows = called(
        logits_kernel,
        [VMEM] * 4 + [ANY],
        [VMEM] * 3 + [ANY] * 3,
        [
            shape((2 * rows, tokens), f32),
            shape((2 * rows, tokens), f32),
            shape((nx * ny, 2, tokens), f32),
            shape((tokens, ds), bf16),
            shape((tokens // 2, ds), bf16),
            shape((tokens // 2, ds), bf16),
        ],
        LOGITS,
        [
            pltpu.VMEM((rows, dt), bf16),
            pltpu.SemaphoreType.DMA((1 + 3 * nx,)),
        ],
    )(plane, teacher_head, student_head, student_other, teacher_other)
    logs = exchanged(logs, PLANE)
    logs = called(merge_kernel, [VMEM], VMEM, shape((nz, 2, tokens), f32), 4)(logs)
    logs = exchanged(logs, Z)

    slope, sent, common = called(
        terms_kernel,
        [SMEM] + [VMEM] * 5 + [ANY] * 3,
        [VMEM] * 3,
        [
            shape((2 * rows, tokens), bf16),
            shape((nx, ny, held, qs + 128), bf16),
            shape((1, tokens), f32),
        ],
        BIG,
        [
            pltpu.VMEM((tokens, ds), bf16),
            pltpu.VMEM((nc, rows, ds), bf16),
            pltpu.SemaphoreType.DMA((3,)),
        ],
    )(place, logs, label, cot, t_logits, s_logits, student_rows, student_head, student_other)
    got = exchanged(sent.reshape(nx * ny, held, qs + 128), PLANE)
    got = called(repack_kernel, [VMEM], VMEM, shape((nz, half, qs + 1024), bf16), 8)(got)
    got, slope = lax.optimization_barrier((got, slope))
    got = exchanged(got, Z)
    slope_other, early_rows, late_rows = lax.optimization_barrier(
        (slope[rows:], early_rows, late_rows)
    )
    rows_other = jnp.concatenate([swapped(early_rows), swapped(late_rows)])

    head_grad = (
        dot(slope[:rows], student_rows, 1, 0)
        + dot(swapped(slope_other), rows_other, 1, 0)
    ).astype(bf16)

    got = called(share_kernel, [VMEM] * 2, VMEM, shape((nx * nc, half, qs + 512), f32), 4)(
        got, common
    )
    got, head_grad = lax.optimization_barrier((exchanged(got, (X, C)), head_grad))
    student_grad, gain_grad, loss = called(
        final_kernel,
        [VMEM] * 3,
        [VMEM] * 3,
        [shape((own, ds), f32), shape((ds // 128, 128), f32), shape((1, 1), f32)],
        4,
        [pltpu.VMEM((ds // 128, 128), f32)],
    )(got, student_hidden, s_gain)
    return (loss.reshape(()), student_grad, gain_grad.reshape(ds), head_grad)


def solution(mesh):
    finer = Mesh(mesh.devices.reshape(4, 2, 16, 4), SECTION_DP)
    placed = (
        P(DP, None),
        P(DP, None),
        P(),
        P(),
        P(SECTION_DP, None),
        P(SECTION_DP, None),
        P(),
        P(),
    )
    return jax.shard_map(
        on_device,
        mesh=finer,
        in_specs=placed,
        out_specs=(P(), P(DP, None), P(), P(SECTION_DP, None)),
        check_vma=False,
    )
```

```python
import jax
import jax.numpy as jnp
from jax import lax
from jax.experimental import pallas as pl
from jax.experimental.pallas import tpu as pltpu
from jax.sharding import Mesh
from jax.sharding import PartitionSpec as P

X, C, Z, Y = ("section_0", "section_1", "dp_0", "dp_1")
DP = (Z, Y)
SECTION_DP = (X, C, Z, Y)
PLANE = (X, Y)

eps = 1e-06
ce_weight = 0.5
f32 = jnp.float32
bf16 = jnp.bfloat16

VMEM = pl.BlockSpec(memory_space=pltpu.VMEM)
SMEM = pl.BlockSpec(memory_space=pltpu.SMEM)
ANY = pl.BlockSpec(memory_space=pl.ANY)
MIB = 2**20
NORM = 63
LOGITS = 52
BIG = 16
shape = jax.ShapeDtypeStruct


def to_all(x, axes):
    length = lax.axis_size(axes)
    return exchanged(jnp.broadcast_to(x[None], (length, *x.shape)), axes)


def exchanged(x, axes):
    return lax.all_to_all(x, axes, 0, 0, tiled=True)


def swapped(x):
    return lax.ppermute(x, C, [(0, 1), (1, 0)])


def dot(a, b, along_a, along_b):
    return lax.dot_general(a, b, (((along_a,), (along_b,)), ((), ())), preferred_element_type=f32)


def column_log(logits):
    peak = jnp.max(logits, axis=0, keepdims=True)
    return peak + jnp.log(jnp.sum(jnp.exp(logits - peak), axis=0, keepdims=True))


def chunk(k):
    return slice(k * 128, (k + 1) * 128)


def called(kernel, in_specs, out_specs, out_shape, mib, scratch=()):
    return pl.pallas_call(
        kernel,
        in_specs=in_specs,
        out_specs=out_specs,
        out_shape=out_shape,
        scratch_shapes=list(scratch),
        compiler_params=pltpu.CompilerParams(vmem_limit_bytes=mib * MIB),
    )


def norm_kernel(
    at_x, at_c, teacher_at, student_at, t_gain_at, s_gain_at, out,
    teacher, student, t_gain, s_gain, t_scaled, s_scaled, gains, sems,
):
    pairs = (
        (teacher_at, teacher),
        (t_gain_at, t_gain),
        (student_at, student),
        (s_gain_at, s_gain),
    )
    copies = [pltpu.make_async_copy(a, b, sems.at[k]) for k, (a, b) in enumerate(pairs)]
    for copy in copies:
        copy.start()
    ix, ic = (at_x[0], at_c[0])
    half = out.shape[1]
    at = 0
    for n, (hidden, gain, scaled) in enumerate(
        ((teacher, t_gain, t_scaled), (student, s_gain, s_scaled))
    ):
        copies[2 * n].wait()
        copies[2 * n + 1].wait()
        values = hidden[...].astype(f32)
        inverse = lax.rsqrt(jnp.mean(values * values, axis=-1, keepdims=True) + eps)
        scaled[...] = values * inverse
        lines = gain.shape[0]
        gains[0:lines] = gain[...].astype(f32)
        width = scaled.shape[1] // 4
        part = scaled[:, pl.ds(pl.multiple_of(ix * width, 128), width)]
        mine = jnp.where(ic == 0, part[0:half], part[half : 2 * half])
        for k in range(width // 128):
            line = gains[pl.ds(ix * (width // 128) + k, 1)]
            normed = (mine[:, chunk(k)] * line).astype(bf16)
            for z in range(out.shape[0]):
                out[z, :, at : at + 128] = normed
            at += 128


def logits_kernel(
    plane, s_own_at, s_other_at, t_own_at, t_other_at,
    t_logits, s_logits, logs, student_rows, early_rows, late_rows,
    s_own, s_other, t_own, t_other, sems, head_sems,
):
    nx, tokens, _ = plane.shape
    rows, dt = t_own_at.shape
    qt = dt // nx
    qs = s_own_at.shape[1] // nx
    heads = (
        (s_own_at, s_own),
        (s_other_at, s_other),
        (t_own_at, t_own),
        (t_other_at, t_other),
    )
    heads = [pltpu.make_async_copy(a, b, head_sems.at[k]) for k, (a, b) in enumerate(heads)]
    for copy in heads:
        copy.start()
    back = []
    for k in range(nx):
        at = slice(k * qs, (k + 1) * qs)
        for n, (target, first, last) in enumerate(
            (
                (student_rows, 0, tokens),
                (early_rows, 0, tokens // 2),
                (late_rows, tokens // 2, tokens),
            )
        ):
            back.append(
                pltpu.make_async_copy(
                    plane.at[k, first:last, qt:], target.at[:, at], sems.at[1 + 3 * k + n]
                )
            )
            back[-1].start()
    for copy, (out, n, head, at, width) in zip(
        heads,
        (
            (s_logits, 0, s_own, qt, qs),
            (s_logits, 1, s_other, qt, qs),
            (t_logits, 0, t_own, 0, qt),
            (t_logits, 1, t_other, 0, qt),
        ),
    ):
        copy.wait()
        total = 0.0
        for k in range(nx):
            part = plane[k, :, at : at + width]
            total += dot(head[:, k * width : (k + 1) * width], part, 1, 1)
        out[n * rows : (n + 1) * rows] = total
    t_log = column_log(t_logits[...])
    s_log = column_log(s_logits[...])
    for k in range(logs.shape[0]):
        logs[k, 0:1] = t_log
        logs[k, 1:2] = s_log
    for copy in back:
        copy.wait()


def merge_kernel(got, out):
    t_log = column_log(got[:, 0, :])
    s_log = column_log(got[:, 1, :])
    for k in range(out.shape[0]):
        out[k, 0:1] = t_log
        out[k, 1:2] = s_log


def terms_kernel(
    place, got, label, cot, t_logits, s_logits, s_rows_at, s_own, s_other,
    slope, sent, common, s_rows, s_heads, sems,
):
    rows = s_own.shape[0]
    pairs = ((s_own, s_heads.at[0]), (s_other, s_heads.at[1]), (s_rows_at, s_rows))
    copies = [pltpu.make_async_copy(a, b, sems.at[k]) for k, (a, b) in enumerate(pairs)]
    for copy in copies:
        copy.start()
    nx, ny, held, _ = sent.shape
    qs = s_rows.shape[1] // nx
    teacher_log = column_log(got[:, 0, :])
    student_log = column_log(got[:, 1, :])
    common[...] = (1.0 + ce_weight) * student_log - teacher_log
    loss_terms = 0.0
    for k in range(2):
        at = slice(k * rows, (k + 1) * rows)
        s_part, t_part = (s_logits[at], t_logits[at])
        entry = lax.broadcasted_iota(jnp.int32, s_part.shape, 0) + place[k]
        hits = entry == label[...]
        s_prob = jnp.exp(s_part - student_log)
        t_prob = jnp.exp(t_part - teacher_log)
        onehot = jnp.where(hits, 1.0, 0.0)
        value = cot[...] * ((1.0 + ce_weight) * s_prob - t_prob - ce_weight * onehot)
        slope[at] = value.astype(bf16)
        lost = t_prob * (t_part - s_part) - ce_weight * jnp.where(hits, s_part, 0.0)
        loss_terms += jnp.sum(lost, axis=0, keepdims=True)
    for copy in copies:
        copy.wait()
    line = lax.broadcasted_iota(jnp.int32, (16, 128), 0)
    loss_high = loss_terms.astype(bf16).astype(f32)
    slopes = slope[...]
    for x in range(nx):
        at = slice(x * qs, (x + 1) * qs)
        terms = dot(slopes[:rows], s_heads[0, :, at], 0, 0)
        terms += dot(slopes[rows:], s_heads[1, :, at], 0, 0)
        gain = jnp.sum(terms * s_rows[:, at].astype(f32), axis=0, keepdims=True)
        high = gain.astype(bf16).astype(f32)
        tail = jnp.where(line == 14, loss_high, jnp.where(line == 15, loss_terms - loss_high, 0.0))
        for k in range(qs // 128):
            tail = jnp.where(line == k, high[:, chunk(k)], tail)
            tail = jnp.where(line == 7 + k, (gain - high)[:, chunk(k)], tail)
        terms = terms.astype(bf16)
        for y in range(ny):
            sent[x, y, :, 0:qs] = terms[y * held : (y + 1) * held]
            sent[x, y, 0:16, qs:] = tail.astype(bf16)
            sent[x, y, 16:held, qs:] = jnp.zeros((held - 16, 128), bf16)


def repack_kernel(got, out):
    total = got[0].astype(f32)
    for k in range(1, got.shape[0]):
        total += got[k].astype(f32)
    nz, half, _ = out.shape
    qs = got.shape[2] - 128
    tail = total[0:16, qs:]
    lines = [tail[k : k + 1] + tail[7 + k : 8 + k] for k in range(7)]
    lines.append(tail[14:15] + tail[15:16])
    pairs = []
    for line in lines:
        high = line.astype(bf16).astype(f32)
        pairs.append(jnp.concatenate([high, line - high], axis=0).astype(bf16))
    for z in range(nz):
        out[z, :, 0:qs] = total[z * half : (z + 1) * half, 0:qs].astype(bf16)
        for k in range(8):
            out[z, :, qs + k * 128 : qs + (k + 1) * 128] = pairs[k]


def share_kernel(got, common, out):
    total = got[0].astype(f32)
    for k in range(1, got.shape[0]):
        total += got[k].astype(f32)
    qs = out.shape[2] - 512
    lines = [total[0:1, qs + k * 128 : qs + (k + 1) * 128] for k in range(8)]
    lines = [x + total[1:2, qs + k * 128 : qs + (k + 1) * 128] for k, x in enumerate(lines)]
    lines[7] += common[...]
    for k in range(out.shape[0]):
        out[k, :, 0:qs] = total[:, 0:qs]
        for n in range(8):
            at = qs + (n % 4) * 128
            out[k, n // 4 : n // 4 + 1, at : at + 128] = lines[n]


def final_kernel(got, hidden, gain, student_grad, gain_grad, loss, gains):
    values = hidden[...].astype(f32)
    own, ds = values.shape
    inverse = lax.rsqrt(jnp.mean(values * values, axis=-1, keepdims=True) + eps)
    scaled = values * inverse
    gains[...] = gain[...].astype(f32)
    each = gain.shape[0] // 4
    qs = each * 128
    inner = 0.0
    weighted = []
    for x in range(4):
        pair = (got[2 * x], got[2 * x + 1])
        for k in range(each):
            line = x * each + k
            grad = jnp.concatenate([p[:, chunk(k)] for p in pair], axis=0)
            weighted.append(grad * gains[line : line + 1])
            inner += jnp.sum(weighted[-1] * scaled[:, chunk(line)], axis=1, keepdims=True)
            row, at = (k // 4, qs + (k % 4) * 128)
            both = sum(p[row : row + 1, at : at + 128] for p in pair)
            gain_grad[line : line + 1] = both / gains[line : line + 1]
    inner = inner * (1.0 / ds)
    for k in range(4 * each):
        student_grad[:, chunk(k)] = inverse * (weighted[k] - scaled[:, chunk(k)] * inner)
    at = qs + 384
    lost = got[0][1:2, at:] + got[1][1:2, at:]
    loss[...] = jnp.sum(lost, axis=1, keepdims=True) * (1.0 / 256)


def on_device(
    teacher_hidden,
    student_hidden,
    teacher_gain,
    student_gain,
    teacher_head,
    student_head,
    labels,
    cotangent,
):
    nx, nc, nz, ny = (lax.axis_size(a) for a in SECTION_DP)
    ix, ic, iz, iy = (lax.axis_index(a) for a in SECTION_DP)
    rows, dt = teacher_head.shape
    own, ds = student_hidden.shape
    half = own // nc
    qt, qs = (dt // nx, ds // nx)
    held = nz * half
    tokens = ny * held

    def start_of(core):
        return (((ix * nc + core) * nz + iz) * ny + iy) * rows

    t_gain, s_gain = (g.reshape(-1, 128) for g in (teacher_gain, student_gain))
    pieces = called(
        norm_kernel,
        [SMEM] * 2 + [ANY] * 4,
        VMEM,
        shape((nz, half, qt + qs), bf16),
        NORM,
        [
            pltpu.VMEM((own, dt), bf16),
            pltpu.VMEM((own, ds), bf16),
            pltpu.VMEM((dt // 128, 128), bf16),
            pltpu.VMEM((ds // 128, 128), bf16),
            pltpu.VMEM((own, dt), f32),
            pltpu.VMEM((own, ds), f32),
            pltpu.VMEM((dt // 128, 128), f32),
            pltpu.SemaphoreType.DMA((4,)),
        ],
    )(ix[None], ic[None], teacher_hidden, student_hidden, t_gain, s_gain)

    def of_tokens(a):
        mine = lax.dynamic_index_in_dim(a.reshape(nz, ny, nc, half), ic, 2, keepdims=False)
        return mine.transpose(1, 0, 2).reshape(1, tokens)

    pieces, labels, cotangent, ix = lax.optimization_barrier((pieces, labels, cotangent, ix))
    label, cot = (of_tokens(labels), of_tokens(cotangent))
    line = exchanged(pieces, Z).reshape(held, qt + qs)
    place = jnp.stack([start_of(ic), start_of(1 - ic)])
    line, place, label, cot, teacher_head, student_head = lax.optimization_barrier(
        (line, place, label, cot, teacher_head, student_head)
    )
    teacher_other, student_other = (swapped(teacher_head), swapped(student_head))
    plane = to_all(line, PLANE).reshape(nx, tokens, qt + qs)

    t_logits, s_logits, logs, student_rows, early_rows, late_rows = called(
        logits_kernel,
        [VMEM] + [ANY] * 4,
        [VMEM] * 3 + [ANY] * 3,
        [
            shape((2 * rows, tokens), f32),
            shape((2 * rows, tokens), f32),
            shape((nx * ny, 2, tokens), f32),
            shape((tokens, ds), bf16),
            shape((tokens // 2, ds), bf16),
            shape((tokens // 2, ds), bf16),
        ],
        LOGITS,
        [
            pltpu.VMEM((rows, ds), bf16),
            pltpu.VMEM((rows, ds), bf16),
            pltpu.VMEM((rows, dt), bf16),
            pltpu.VMEM((rows, dt), bf16),
            pltpu.SemaphoreType.DMA((1 + 3 * nx,)),
            pltpu.SemaphoreType.DMA((4,)),
        ],
    )(plane, student_head, student_other, teacher_head, teacher_other)
    logs = exchanged(logs, PLANE)
    logs = called(merge_kernel, [VMEM], VMEM, shape((nz, 2, tokens), f32), 4)(logs)
    logs = exchanged(logs, Z)

    slope, sent, common = called(
        terms_kernel,
        [SMEM] + [VMEM] * 5 + [ANY] * 3,
        [VMEM] * 3,
        [
            shape((2 * rows, tokens), bf16),
            shape((nx, ny, held, qs + 128), bf16),
            shape((1, tokens), f32),
        ],
        BIG,
        [
            pltpu.VMEM((tokens, ds), bf16),
            pltpu.VMEM((nc, rows, ds), bf16),
            pltpu.SemaphoreType.DMA((3,)),
        ],
    )(place, logs, label, cot, t_logits, s_logits, student_rows, student_head, student_other)
    got = exchanged(sent.reshape(nx * ny, held, qs + 128), PLANE)
    got = called(repack_kernel, [VMEM], VMEM, shape((nz, half, qs + 1024), bf16), 8)(got)
    got, slope = lax.optimization_barrier((got, slope))
    got = exchanged(got, Z)
    slope_other, early_rows, late_rows = lax.optimization_barrier(
        (slope[rows:], early_rows, late_rows)
    )
    rows_other = jnp.concatenate([swapped(early_rows), swapped(late_rows)])

    head_grad = (
        dot(slope[:rows], student_rows, 1, 0)
        + dot(swapped(slope_other), rows_other, 1, 0)
    ).astype(bf16)

    got = called(share_kernel, [VMEM] * 2, VMEM, shape((nx * nc, half, qs + 512), f32), 4)(
        got, common
    )
    got, head_grad = lax.optimization_barrier((exchanged(got, (X, C)), head_grad))
    student_grad, gain_grad, loss = called(
        final_kernel,
        [VMEM] * 3,
        [VMEM] * 3,
        [shape((own, ds), f32), shape((ds // 128, 128), f32), shape((1, 1), f32)],
        4,
        [pltpu.VMEM((ds // 128, 128), f32)],
    )(got, student_hidden, s_gain)
    return (loss.reshape(()), student_grad, gain_grad.reshape(ds), head_grad)


def solution(mesh):
    finer = Mesh(mesh.devices.reshape(4, 2, 16, 4), SECTION_DP)
    placed = (
        P(DP, None),
        P(DP, None),
        P(),
        P(),
        P(SECTION_DP, None),
        P(SECTION_DP, None),
        P(),
        P(),
    )
    return jax.shard_map(
        on_device,
        mesh=finer,
        in_specs=placed,
        out_specs=(P(), P(DP, None), P(), P(SECTION_DP, None)),
        check_vma=False,
    )
```

```python
import jax
import jax.numpy as jnp
from jax import lax
from jax.experimental import pallas as pl
from jax.experimental.pallas import tpu as pltpu
from jax.sharding import Mesh
from jax.sharding import PartitionSpec as P

X, C, Z, Y = ("section_0", "section_1", "dp_0", "dp_1")
DP = (Z, Y)
SECTION_DP = (X, C, Z, Y)
PLANE = (X, Y)

eps = 1e-06
ce_weight = 0.5
f32 = jnp.float32
bf16 = jnp.bfloat16

VMEM = pl.BlockSpec(memory_space=pltpu.VMEM)
SMEM = pl.BlockSpec(memory_space=pltpu.SMEM)
ANY = pl.BlockSpec(memory_space=pl.ANY)
MIB = 2**20
NORM = 63
LOGITS = 10
BIG = 16
shape = jax.ShapeDtypeStruct


def to_all(x, axes):
    length = lax.axis_size(axes)
    return exchanged(jnp.broadcast_to(x[None], (length, *x.shape)), axes)


def exchanged(x, axes):
    return lax.all_to_all(x, axes, 0, 0, tiled=True)


def swapped(x):
    return lax.ppermute(x, C, [(0, 1), (1, 0)])


def dot(a, b, along_a, along_b):
    return lax.dot_general(a, b, (((along_a,), (along_b,)), ((), ())), preferred_element_type=f32)


def column_log(logits):
    peak = jnp.max(logits, axis=0, keepdims=True)
    return peak + jnp.log(jnp.sum(jnp.exp(logits - peak), axis=0, keepdims=True))


def chunk(k):
    return slice(k * 128, (k + 1) * 128)


def called(kernel, in_specs, out_specs, out_shape, mib, scratch=()):
    return pl.pallas_call(
        kernel,
        in_specs=in_specs,
        out_specs=out_specs,
        out_shape=out_shape,
        scratch_shapes=list(scratch),
        compiler_params=pltpu.CompilerParams(vmem_limit_bytes=mib * MIB),
    )


def norm_kernel(
    at_x, at_c, teacher_at, student_at, t_gain_at, s_gain_at, out,
    teacher, student, t_gain, s_gain, t_scaled, s_scaled, gains, sems,
):
    pairs = (
        (teacher_at, teacher),
        (t_gain_at, t_gain),
        (student_at, student),
        (s_gain_at, s_gain),
    )
    copies = [pltpu.make_async_copy(a, b, sems.at[k]) for k, (a, b) in enumerate(pairs)]
    for copy in copies:
        copy.start()
    ix, ic = (at_x[0], at_c[0])
    half = out.shape[1]
    at = 0
    for n, (hidden, gain, scaled) in enumerate(
        ((teacher, t_gain, t_scaled), (student, s_gain, s_scaled))
    ):
        copies[2 * n].wait()
        copies[2 * n + 1].wait()
        values = hidden[...].astype(f32)
        inverse = lax.rsqrt(jnp.mean(values * values, axis=-1, keepdims=True) + eps)
        scaled[...] = values * inverse
        lines = gain.shape[0]
        gains[0:lines] = gain[...].astype(f32)
        width = scaled.shape[1] // 4
        part = scaled[:, pl.ds(pl.multiple_of(ix * width, 128), width)]
        mine = jnp.where(ic == 0, part[0:half], part[half : 2 * half])
        for k in range(width // 128):
            line = gains[pl.ds(ix * (width // 128) + k, 1)]
            normed = (mine[:, chunk(k)] * line).astype(bf16)
            for z in range(out.shape[0]):
                out[z, :, at : at + 128] = normed
            at += 128


def logits_kernel(
    plane, t_own, s_own, s_other, t_other_at,
    t_logits, s_logits, logs, student_rows, t_other, sems,
):
    nx = plane.shape[0]
    rows, dt = t_own.shape
    qt = dt // nx
    qs = s_own.shape[1] // nx
    late = pltpu.make_async_copy(t_other_at, t_other, sems.at[0])
    late.start()
    back = [
        pltpu.make_async_copy(
            plane.at[k, :, qt:], student_rows.at[:, k * qs : (k + 1) * qs], sems.at[1 + k]
        )
        for k in range(nx)
    ]
    for out, n, head, at, width in (
        (s_logits, 0, s_own, qt, qs),
        (s_logits, 1, s_other, qt, qs),
        (t_logits, 0, t_own, 0, qt),
        (t_logits, 1, t_other, 0, qt),
    ):
        if head is t_own:
            for copy in back:
                copy.start()
        if head is t_other:
            late.wait()
        total = 0.0
        for k in range(nx):
            part = plane[k, :, at : at + width]
            total += dot(head[:, k * width : (k + 1) * width], part, 1, 1)
        out[n * rows : (n + 1) * rows] = total
    t_log = column_log(t_logits[...])
    s_log = column_log(s_logits[...])
    for k in range(logs.shape[0]):
        logs[k, 0:1] = t_log
        logs[k, 1:2] = s_log
    for copy in back:
        copy.wait()


def merge_kernel(got, out):
    t_log = column_log(got[:, 0, :])
    s_log = column_log(got[:, 1, :])
    for k in range(out.shape[0]):
        out[k, 0:1] = t_log
        out[k, 1:2] = s_log


def terms_kernel(
    place, got, label, cot, t_logits, s_logits, s_rows_at, s_own, s_other,
    slope, sent, common, s_rows, s_heads, sems,
):
    rows = s_own.shape[0]
    pairs = ((s_own, s_heads.at[0]), (s_other, s_heads.at[1]), (s_rows_at, s_rows))
    copies = [pltpu.make_async_copy(a, b, sems.at[k]) for k, (a, b) in enumerate(pairs)]
    for copy in copies:
        copy.start()
    nx, ny, held, _ = sent.shape
    qs = s_rows.shape[1] // nx
    teacher_log = column_log(got[:, 0, :])
    student_log = column_log(got[:, 1, :])
    common[...] = (1.0 + ce_weight) * student_log - teacher_log
    loss_terms = 0.0
    for k in range(2):
        at = slice(k * rows, (k + 1) * rows)
        s_part, t_part = (s_logits[at], t_logits[at])
        entry = lax.broadcasted_iota(jnp.int32, s_part.shape, 0) + place[k]
        hits = entry == label[...]
        s_prob = jnp.exp(s_part - student_log)
        t_prob = jnp.exp(t_part - teacher_log)
        onehot = jnp.where(hits, 1.0, 0.0)
        value = cot[...] * ((1.0 + ce_weight) * s_prob - t_prob - ce_weight * onehot)
        slope[at] = value.astype(bf16)
        lost = t_prob * (t_part - s_part) - ce_weight * jnp.where(hits, s_part, 0.0)
        loss_terms += jnp.sum(lost, axis=0, keepdims=True)
    for copy in copies:
        copy.wait()
    line = lax.broadcasted_iota(jnp.int32, (16, 128), 0)
    loss_high = loss_terms.astype(bf16).astype(f32)
    slopes = slope[...]
    for x in range(nx):
        at = slice(x * qs, (x + 1) * qs)
        terms = dot(slopes[:rows], s_heads[0, :, at], 0, 0)
        terms += dot(slopes[rows:], s_heads[1, :, at], 0, 0)
        gain = jnp.sum(terms * s_rows[:, at].astype(f32), axis=0, keepdims=True)
        high = gain.astype(bf16).astype(f32)
        tail = jnp.where(line == 14, loss_high, jnp.where(line == 15, loss_terms - loss_high, 0.0))
        for k in range(qs // 128):
            tail = jnp.where(line == k, high[:, chunk(k)], tail)
            tail = jnp.where(line == 7 + k, (gain - high)[:, chunk(k)], tail)
        terms = terms.astype(bf16)
        for y in range(ny):
            sent[x, y, :, 0:qs] = terms[y * held : (y + 1) * held]
            sent[x, y, 0:16, qs:] = tail.astype(bf16)
            sent[x, y, 16:held, qs:] = jnp.zeros((held - 16, 128), bf16)


def repack_kernel(got, out):
    total = got[0].astype(f32)
    for k in range(1, got.shape[0]):
        total += got[k].astype(f32)
    nz, half, _ = out.shape
    qs = got.shape[2] - 128
    tail = total[0:16, qs:]
    lines = [tail[k : k + 1] + tail[7 + k : 8 + k] for k in range(7)]
    lines.append(tail[14:15] + tail[15:16])
    pairs = []
    for line in lines:
        high = line.astype(bf16).astype(f32)
        pairs.append(jnp.concatenate([high, line - high], axis=0).astype(bf16))
    for z in range(nz):
        out[z, :, 0:qs] = total[z * half : (z + 1) * half, 0:qs].astype(bf16)
        for k in range(8):
            out[z, :, qs + k * 128 : qs + (k + 1) * 128] = pairs[k]


def share_kernel(got, common, out):
    total = got[0].astype(f32)
    for k in range(1, got.shape[0]):
        total += got[k].astype(f32)
    qs = out.shape[2] - 512
    lines = [total[0:1, qs + k * 128 : qs + (k + 1) * 128] for k in range(8)]
    lines = [x + total[1:2, qs + k * 128 : qs + (k + 1) * 128] for k, x in enumerate(lines)]
    lines[7] += common[...]
    for k in range(out.shape[0]):
        out[k, :, 0:qs] = total[:, 0:qs]
        for n in range(8):
            at = qs + (n % 4) * 128
            out[k, n // 4 : n // 4 + 1, at : at + 128] = lines[n]


def final_kernel(got, hidden, gain, student_grad, gain_grad, loss, gains):
    values = hidden[...].astype(f32)
    own, ds = values.shape
    inverse = lax.rsqrt(jnp.mean(values * values, axis=-1, keepdims=True) + eps)
    scaled = values * inverse
    gains[...] = gain[...].astype(f32)
    each = gain.shape[0] // 4
    qs = each * 128
    inner = 0.0
    weighted = []
    for x in range(4):
        pair = (got[2 * x], got[2 * x + 1])
        for k in range(each):
            line = x * each + k
            grad = jnp.concatenate([p[:, chunk(k)] for p in pair], axis=0)
            weighted.append(grad * gains[line : line + 1])
            inner += jnp.sum(weighted[-1] * scaled[:, chunk(line)], axis=1, keepdims=True)
            row, at = (k // 4, qs + (k % 4) * 128)
            both = sum(p[row : row + 1, at : at + 128] for p in pair)
            gain_grad[line : line + 1] = both / gains[line : line + 1]
    inner = inner * (1.0 / ds)
    for k in range(4 * each):
        student_grad[:, chunk(k)] = inverse * (weighted[k] - scaled[:, chunk(k)] * inner)
    at = qs + 384
    lost = got[0][1:2, at:] + got[1][1:2, at:]
    loss[...] = jnp.sum(lost, axis=1, keepdims=True) * (1.0 / 256)


def on_device(
    teacher_hidden,
    student_hidden,
    teacher_gain,
    student_gain,
    teacher_head,
    student_head,
    labels,
    cotangent,
):
    nx, nc, nz, ny = (lax.axis_size(a) for a in SECTION_DP)
    ix, ic, iz, iy = (lax.axis_index(a) for a in SECTION_DP)
    rows, dt = teacher_head.shape
    own, ds = student_hidden.shape
    half = own // nc
    qt, qs = (dt // nx, ds // nx)
    held = nz * half
    tokens = ny * held

    def start_of(core):
        return (((ix * nc + core) * nz + iz) * ny + iy) * rows

    t_gain, s_gain = (g.reshape(-1, 128) for g in (teacher_gain, student_gain))
    pieces = called(
        norm_kernel,
        [SMEM] * 2 + [ANY] * 4,
        VMEM,
        shape((nz, half, qt + qs), bf16),
        NORM,
        [
            pltpu.VMEM((own, dt), bf16),
            pltpu.VMEM((own, ds), bf16),
            pltpu.VMEM((dt // 128, 128), bf16),
            pltpu.VMEM((ds // 128, 128), bf16),
            pltpu.VMEM((own, dt), f32),
            pltpu.VMEM((own, ds), f32),
            pltpu.VMEM((dt // 128, 128), f32),
            pltpu.SemaphoreType.DMA((4,)),
        ],
    )(ix[None], ic[None], teacher_hidden, student_hidden, t_gain, s_gain)

    def of_tokens(a):
        mine = lax.dynamic_index_in_dim(a.reshape(nz, ny, nc, half), ic, 2, keepdims=False)
        return mine.transpose(1, 0, 2).reshape(1, tokens)

    pieces, labels, cotangent, ix = lax.optimization_barrier((pieces, labels, cotangent, ix))
    label, cot = (of_tokens(labels), of_tokens(cotangent))
    pieces, teacher_head, student_head = lax.optimization_barrier(
        (pieces, teacher_head, student_head)
    )
    teacher_other, student_other = (swapped(teacher_head), swapped(student_head))

    line = exchanged(pieces, Z).reshape(held, qt + qs)
    place = jnp.stack([start_of(ic), start_of(1 - ic)])
    line, place, label, cot, teacher_other, student_other = lax.optimization_barrier(
        (line, place, label, cot, teacher_other, student_other)
    )
    plane = to_all(line, PLANE).reshape(nx, tokens, qt + qs)

    t_logits, s_logits, logs, student_rows = called(
        logits_kernel,
        [VMEM] * 4 + [ANY],
        [VMEM] * 3 + [ANY],
        [
            shape((2 * rows, tokens), f32),
            shape((2 * rows, tokens), f32),
            shape((nx * ny, 2, tokens), f32),
            shape((tokens, ds), bf16),
        ],
        LOGITS,
        [
            pltpu.VMEM((rows, dt), bf16),
            pltpu.SemaphoreType.DMA((1 + nx,)),
        ],
    )(plane, teacher_head, student_head, student_other, teacher_other)
    logs = exchanged(logs, PLANE)
    logs = called(merge_kernel, [VMEM], VMEM, shape((nz, 2, tokens), f32), 4)(logs)
    logs = exchanged(logs, Z)

    slope, sent, common = called(
        terms_kernel,
        [SMEM] + [VMEM] * 5 + [ANY] * 3,
        [VMEM] * 3,
        [
            shape((2 * rows, tokens), bf16),
            shape((nx, ny, held, qs + 128), bf16),
            shape((1, tokens), f32),
        ],
        BIG,
        [
            pltpu.VMEM((tokens, ds), bf16),
            pltpu.VMEM((nc, rows, ds), bf16),
            pltpu.SemaphoreType.DMA((3,)),
        ],
    )(place, logs, label, cot, t_logits, s_logits, student_rows, student_head, student_other)
    got = exchanged(sent.reshape(nx * ny, held, qs + 128), PLANE)
    got = called(repack_kernel, [VMEM], VMEM, shape((nz, half, qs + 1024), bf16), 8)(got)
    got, slope = lax.optimization_barrier((got, slope))
    got = exchanged(got, Z)
    slope_other, student_rows = lax.optimization_barrier((slope[rows:], student_rows))
    cut = tokens // 2
    rows_other = jnp.concatenate([swapped(student_rows[:cut]), swapped(student_rows[cut:])])

    head_grad = (
        dot(slope[:rows], student_rows, 1, 0)
        + dot(swapped(slope_other), rows_other, 1, 0)
    ).astype(bf16)

    got = called(share_kernel, [VMEM] * 2, VMEM, shape((nx * nc, half, qs + 512), f32), 4)(
        got, common
    )
    got, head_grad = lax.optimization_barrier((exchanged(got, (X, C)), head_grad))
    student_grad, gain_grad, loss = called(
        final_kernel,
        [VMEM] * 3,
        [VMEM] * 3,
        [shape((own, ds), f32), shape((ds // 128, 128), f32), shape((1, 1), f32)],
        4,
        [pltpu.VMEM((ds // 128, 128), f32)],
    )(got, student_hidden, s_gain)
    return (loss.reshape(()), student_grad, gain_grad.reshape(ds), head_grad)


def solution(mesh):
    finer = Mesh(mesh.devices.reshape(4, 2, 16, 4), SECTION_DP)
    placed = (
        P(DP, None),
        P(DP, None),
        P(),
        P(),
        P(SECTION_DP, None),
        P(SECTION_DP, None),
        P(),
        P(),
    )
    return jax.shard_map(
        on_device,
        mesh=finer,
        in_specs=placed,
        out_specs=(P(), P(DP, None), P(), P(SECTION_DP, None)),
        check_vma=False,
    )
```
